32 devices in a mesh: rows: 8 (over z, y), blk: 4 (over x, core).
Axes of the slice: x: 2, y: 2, z: 4, core: 2. Of those that a mesh axis runs over, the one named last changes fastest.
Arguments:
- features: bfloat16 [8192, 1024], P(('rows', 'blk')), may hold values from -6 to 6
- tiles: bfloat16 [32, 3, 256, 256], P(('rows', 'blk')), may hold values from -0.1875 to 0.1875
- tile_cols: int32 [32, 3], P(('rows', 'blk')), may hold values from 0 to 31, as said below
- tile_count: int32 [32], P(('rows', 'blk')), may hold values from 1 to 3
- weight: bfloat16 [1024, 1024], P(('rows', 'blk')), may hold values from -0.1875 to 0.1875
- cotangent: bfloat16 [8192, 1024], P(('rows', 'blk')), may hold values from -0.125 to 0.125
Outputs:
- output: bfloat16 [8192, 1024], P(('rows', 'blk'))
- weight_grad: float32 [1024, 1024], P(('rows', 'blk'))
The draws below stay inside these ranges and needn't reach their ends.
Inputs may be any that keep to these rules, and one draw needn't show every extreme that they name: For each row block g, the first tile_count[g] entries of tile_cols[g] are distinct blocks of g's group of 4 blocks (blocks 4 * (g // 4) onward), each at most 1 positions from g around that group, g itself among them; the later entries are also blocks of that group and carry no tile.
All inputs are finite; a program needn't handle non-finite values.
Results may differ from the reference program's by a relative error of at most 0.0054.
Values may be sent and summed in bfloat16 or wider, within the bound.
No kernel may reach another device: no remote copies, remote signals or barrier semaphores. Data moves between devices by JAX's collectives and lax.ppermute only.
A program may use at most 64 MiB of HBM per device.

```python
import jax
import jax.numpy as jnp
from jax import lax

TILE = 256
F = 1024
CYCLE = 4
REACH = 1
TCAP = 3
NBLK = 32
NODES = 8192


def tile_layout(key):
    base = jax.random.fold_in(key, 7)
    key_level, key_rolls = jax.random.split(base, 2)
    level = jax.random.randint(key_level, (NBLK,), 0, 9)
    rolls = jax.random.randint(key_rolls, (NBLK, 2 * REACH), 0, 81)
    bits = (rolls < (level * level)[:, None]).astype(jnp.int32)
    block_ids = jnp.arange(NBLK, dtype=jnp.int32)
    bits = jnp.where(block_ids[:, None] == 0, 1, bits)
    bits = jnp.where(block_ids[:, None] == 1, 0, bits)
    live_all = jnp.concatenate([jnp.ones((NBLK, 1), jnp.int32), bits], axis=1)
    offsets = jnp.concatenate([jnp.zeros((1,), jnp.int32), jnp.arange(-REACH, 0, dtype=jnp.int32), jnp.arange(1, REACH + 1, dtype=jnp.int32)])
    score = (1 - live_all) * TCAP + jnp.arange(TCAP, dtype=jnp.int32)[None, :]
    order = jnp.argsort(score, axis=1, stable=True)
    sorted_off = offsets[order]
    counts = jnp.sum(live_all, axis=1)
    group = block_ids // CYCLE
    local = block_ids % CYCLE
    columns = group[:, None] * CYCLE + (local[:, None] + sorted_off + CYCLE) % CYCLE
    return (columns.astype(jnp.int32), counts.astype(jnp.int32))


def draw_tile_cols(key, part):
    return tile_layout(key)[0]


def draw_tile_count(key, part):
    return tile_layout(key)[1]


def raised(entries, own_key, source, target, parts, factor):
    owner, partner = [(jnp.arange(entries.shape[position]) // (entries.shape[position] // parts)).reshape([-1 if axis == position else 1 for axis in range(entries.ndim)]) for position in (source, target)]
    chosen = jax.random.permutation(own_key, parts)[partner]
    strong = (owner == chosen) | (owner == (partner + parts // 2) % parts)
    return jnp.where(strong, factor * entries, entries)


def level_of(own_key, dims, cuts, low, largest):
    level = 1.0
    for axis_at, shards_of in cuts:
        heights = jax.random.uniform(jax.random.fold_in(jax.random.fold_in(own_key, 6), axis_at), (shards_of,), jnp.float32, low / len(cuts), largest / len(cuts))
        level = level * jnp.repeat(jnp.exp(heights), dims[axis_at] // shards_of).reshape((-1,) + (1,) * (len(dims) - 1 - axis_at))
    return level


def scatter_about(own_key, shape, width, bound, pieces=(), held_as=jnp.bfloat16):
    gain = level_of(own_key, shape, pieces, -0.22, 0.18) if pieces else 1.0
    result = jax.random.normal(own_key, shape, jnp.float32) * width * gain
    return jnp.minimum(jnp.maximum(result, -bound), bound).astype(held_as)


def gaussian_with(own_key, extent, scale, bound, pieces, heavy, kind=jnp.bfloat16):
    drawn = scale * jax.random.normal(own_key, extent, jnp.float32)
    if pieces:
        drawn = drawn * level_of(own_key, extent, pieces, -0.22, 0.18)
    return jnp.clip(raised(drawn, jax.random.fold_in(own_key, 3), *heavy), -bound, bound).astype(kind)


def setup_inputs(seed: int = 0) -> dict:
    streams_of = jax.random.split(jax.random.key(seed), 7)
    features = scatter_about(streams_of[0], (NODES, F), 1.0, 6.0, ((0, 32),))
    tiles = scatter_about(streams_of[1], (NBLK, TCAP, TILE, TILE), (TILE * 4) ** -0.5, 0.1875, ((0, 32),))
    tile_cols = draw_tile_cols(jax.random.fold_in(streams_of[6], 71), 0)
    tile_count = draw_tile_count(jax.random.fold_in(streams_of[6], 71), 0)
    weight = scatter_about(streams_of[4], (F, F), F ** -0.5, 0.1875, ((0, 32),))
    cotangent = gaussian_with(streams_of[5], (NODES, F), NODES ** -0.5, 0.125, ((0, 32),), (0, 1, 32, 2.75))
    return {"features": features, "tiles": tiles, "tile_cols": tile_cols, "tile_count": tile_count, "weight": weight, "cotangent": cotangent}


def reference(features, tiles, tile_cols, tile_count, weight, cotangent):
    blocks = features.reshape(NBLK, TILE, F)
    slot_ids = jnp.arange(TCAP, dtype=jnp.int32)

    def per_block(block_no):
        columns = tile_cols[block_no]
        gathered = blocks[columns].astype(jnp.float32)
        in_use = (slot_ids < tile_count[block_no]).astype(jnp.float32)
        products = jnp.einsum("kij,kjf->kif", tiles[block_no].astype(jnp.float32), gathered)
        return jnp.einsum("k,kif->if", in_use, products)

    summed = lax.map(per_block, jnp.arange(NBLK, dtype=jnp.int32))
    aggregated = summed.reshape(NODES, F).astype(jnp.bfloat16)
    pre_act = jnp.dot(aggregated, weight.T, preferred_element_type=jnp.float32)
    output = jax.nn.silu(pre_act).astype(jnp.bfloat16)
    sigmoid_y = jax.nn.sigmoid(pre_act)
    grad_pre = (cotangent.astype(jnp.float32) * sigmoid_y * (1.0 + pre_act * (1.0 - sigmoid_y))).astype(jnp.bfloat16)
    weight_grad = jnp.dot(grad_pre.T, aggregated, preferred_element_type=jnp.float32)
    return output, weight_grad
```

```python
import jax
import jax.numpy as jnp
from jax import lax
from jax.experimental import pallas as pl
from jax.experimental.pallas import tpu as pltpu
from jax.sharding import PartitionSpec as P

AXES = ("rows", "blk")
CORE = 1
F32 = jnp.float32
BF16 = jnp.bfloat16


def swap(value, mask):
    total = lax.axis_size(AXES)
    return lax.ppermute(value, AXES, [(i, i ^ mask) for i in range(total)])


def shifted(value, by):
    length = lax.axis_size("blk")
    return lax.ppermute(value, "blk", [(i, (i + by) % length) for i in range(length)])


def neighbour_blocks(features, reach):
    length = lax.axis_size("blk")
    position = lax.axis_index("blk")
    if length == 4 and reach == 1:
        return [(position ^ 3, swap(features, 3)), (position ^ 1, swap(features, 1))]
    found = []
    for offset in range(1, reach + 1):
        found.append(((position - offset) % length, shifted(features, offset)))
        found.append(((position + offset) % length, shifted(features, -offset)))
    return found


def gather_weight(weight):
    total = lax.axis_size(AXES)
    if total == 32:
        x, y, z = 2, 4, (8, 16, 24)
        pair = jnp.concatenate([weight, swap(weight, x)])
        along = [pair] + [swap(pair, m) for m in z]
        near = swap(jnp.concatenate(along[:2]), y)
        far = swap(jnp.concatenate(along[2:]), y)
        masks = [b * x + c * y + a * 8 for c in range(2) for a in range(4) for b in range(2)]
        return along + [near, far], masks
    held = weight
    bit = 2
    while bit < total:
        held = jnp.concatenate([held, swap(held, bit)])
        bit *= 2
    return [held], [2 * s for s in range(total // 2)]


def one_hot_rows(me, masks, rows, width):
    owner = jnp.repeat(jnp.asarray(masks, jnp.int32) ^ me, rows)
    at = owner * rows + jnp.tile(jnp.arange(rows, dtype=jnp.int32), len(masks))
    return (at[:, None] == jnp.arange(width, dtype=jnp.int32)[None, :]).astype(BF16)


def layer_kernel(n_pieces, rows, split, *refs):
    agg_own, agg_other, cot_own, cot_other = refs[:4]
    pieces = refs[4 : 4 + n_pieces]
    out_own, out_other = refs[4 + n_pieces : 6 + n_pieces]
    grads = refs[6 + n_pieces : -2]
    w_all, a_all = refs[-2:]
    nodes = agg_own.shape[0]
    at = 0
    for piece in pieces:
        w_all[at : at + piece.shape[0], :] = piece[...]
        at += piece.shape[0]
    a_all[:nodes, :] = agg_own[...]
    a_all[nodes:, :] = agg_other[...]
    step = 128
    for first in range(0, w_all.shape[0], step):
        part = pl.ds(first, step)
        pre = lax.dot_general(
            w_all[part, :], a_all[...], (((1,), (1,)), ((), ())), preferred_element_type=F32
        )
        s = jax.nn.sigmoid(pre)
        out = (pre * s).astype(BF16)
        out_own[part, :] = out[:, :nodes]
        out_other[part, :] = out[:, nodes:]
        slope = s * (1.0 + pre * (1.0 - s))
        gp_own = (cot_own[part, :].astype(F32) * slope[:, :nodes]).astype(BF16)
        gp_other = (cot_other[part, :].astype(F32) * slope[:, nodes:]).astype(BF16)
        grad = jnp.dot(
            jnp.concatenate([gp_own, gp_other], axis=1), a_all[...], preferred_element_type=F32
        )
        if split is None:
            grads[0][part, :] = grad
            continue
        for k in range(step // rows):
            slot = first // rows + k
            p, z = slot // 8 * 2 + slot % 2, slot // 2 % 4
            value = grad[k * rows : (k + 1) * rows, :]
            to_a, to_c = pl.ds(z * rows, rows), pl.ds(p * rows, rows)
            grads[p][to_a, :] = value[:, :split].astype(grads[p].dtype)
            grads[4 + z][to_c, :] = value[:, split:].astype(grads[4 + z].dtype)


def layer(agg_own, agg_other, cot_own, cot_other, pieces, rows, split):
    nodes, width = agg_own.shape
    outs = cot_own.shape[0]
    shapes = [jax.ShapeDtypeStruct((outs, nodes), BF16)] * 2
    if split is None:
        shapes.append(jax.ShapeDtypeStruct((outs, width), F32))
    else:
        for columns in (split, width - split):
            for k in range(4):
                shapes.append(jax.ShapeDtypeStruct((4 * rows, columns), BF16 if k else F32))
    n_in = 4 + len(pieces)

    def body(*refs):
        layer_kernel(len(pieces), rows, split, *refs)

    in_vmem = pl.BlockSpec(memory_space=pltpu.VMEM)
    return pl.pallas_call(
        body,
        out_shape=shapes,
        in_specs=[in_vmem] * n_in,
        out_specs=[in_vmem] * len(shapes),
        scratch_shapes=[pltpu.VMEM((outs, width), BF16), pltpu.VMEM((2 * nodes, width), BF16)],
        compiler_params=pltpu.CompilerParams(vmem_limit_bytes=24 * 1024 * 1024),
        name="layer",
    )(agg_own, agg_other, cot_own, cot_other, *pieces)


def reduce_pieces(grads, rows):
    xy, z = (2, 4, 6), (8, 16, 24)
    a_in = [swap(grads[k], xy[k - 1]) for k in (1, 2, 3)]
    c_in = [swap(grads[4 + k], z[k - 1]) for k in (1, 2, 3)]
    a = grads[0] + sum(v.astype(F32) for v in a_in)
    c = grads[4] + sum(v.astype(F32) for v in c_in)
    a = a.reshape(4, rows, -1)
    c = c.reshape(4, rows, -1)
    a_in = [swap(a[k].astype(BF16), z[k - 1]) for k in (1, 2, 3)]
    c_in = [swap(c[k].astype(BF16), xy[k - 1]) for k in (1, 2, 3)]
    a = a[0] + sum(v.astype(F32) for v in a_in)
    c = c[0] + sum(v.astype(F32) for v in c_in)
    return jnp.concatenate([a, c], axis=1)


def reduce_halving(grad):
    bit = lax.axis_size(AXES) // 2
    while bit > 1:
        half = grad.shape[0] // 2
        grad = grad[:half] + swap(grad[half:].astype(BF16), bit).astype(F32)
        bit //= 2
    return grad


def local(features, tiles, tile_cols, tile_count, weight, cotangent):
    total = lax.axis_size(AXES)
    group_len = lax.axis_size("blk")
    position = lax.axis_index("blk")
    me = lax.axis_index(AXES)
    slot_total = tiles.shape[1]
    rows, width = weight.shape
    slot_ids = jnp.arange(slot_total, dtype=jnp.int32)
    in_use = slot_ids < tile_count[0]
    columns = tile_cols[0] % group_len

    def tile_of(source):
        match = jnp.logical_and(in_use, columns == source)
        return jnp.sum(jnp.where(match[:, None, None], tiles[0], 0), axis=0, dtype=BF16)

    pieces, masks = gather_weight(weight)
    blocks = neighbour_blocks(features, (slot_total - 1) // 2)

    mine = one_hot_rows(me, masks, rows, width)
    others = one_hot_rows(me ^ CORE, masks, rows, width)
    turn = (((1,), (1,)), ((), ()))
    cot_own = lax.dot_general(mine, cotangent, turn, preferred_element_type=F32).astype(BF16)
    cot_other = swap(
        lax.dot_general(others, cotangent, turn, preferred_element_type=F32).astype(BF16), CORE
    )

    summed = jnp.dot(tile_of(position), features, preferred_element_type=F32)
    for source, block in blocks[::-1]:
        summed = summed + jnp.dot(tile_of(source), block, preferred_element_type=F32)
    agg_own = summed.astype(BF16)
    agg_other = swap(agg_own, CORE)

    split = 640 if total == 32 and width == 1024 else None
    out_own, out_other, *grads = layer(
        agg_own, agg_other, cot_own, cot_other, pieces, rows, split
    )
    if split is None:
        weight_grad = reduce_halving(grads[0])
    else:
        weight_grad = reduce_pieces(grads, rows)

    out_t = jnp.concatenate([out_own, swap(out_other, CORE)])
    place = jnp.concatenate([mine, others])
    output = lax.dot_general(
        out_t, place, (((0,), (0,)), ((), ())), preferred_element_type=F32
    ).astype(BF16)
    return output, weight_grad


def solution(mesh):
    in_specs = (
        P(AXES, None),
        P(AXES, None, None, None),
        P(AXES, None),
        P(AXES),
        P(AXES, None),
        P(AXES, None),
    )
    out_specs = (P(AXES, None), P(AXES, None))
    return jax.shard_map(local, mesh=mesh, in_specs=in_specs, out_specs=out_specs, check_vma=False)
```

```python
import jax
import jax.numpy as jnp
from jax import lax
from jax.experimental import pallas as pl
from jax.experimental.pallas import tpu as pltpu
from jax.sharding import PartitionSpec as P

AXES = ("rows", "blk")
CORE, X, Y, NEAR, FAR = 1, 2, 4, 8, 16
ALONG_Z = (0, NEAR, NEAR ^ FAR, FAR)
F32 = jnp.float32
BF16 = jnp.bfloat16
TURN = (((1,), (1,)), ((), ()))
IN_VMEM = pl.BlockSpec(memory_space=pltpu.VMEM)
IN_SMEM = pl.BlockSpec(memory_space=pltpu.SMEM)
LIMIT = pltpu.CompilerParams(vmem_limit_bytes=24 * 1024 * 1024)
BRIEF = pl.CostEstimate(flops=0, bytes_accessed=0, transcendentals=0)
LONG = pl.CostEstimate(flops=20_000_000_000, bytes_accessed=0, transcendentals=0)


def swap(value, mask, odd_mask=None):
    total = lax.axis_size(AXES)
    masks = (mask, mask if odd_mask is None else odd_mask)
    return lax.ppermute(value, AXES, [(i, i ^ masks[i % 2]) for i in range(total)])


def after(value, *earlier):
    return lax.optimization_barrier((value, *earlier))[0]


def shifted(value, by):
    length = lax.axis_size("blk")
    return lax.ppermute(value, "blk", [(i, (i + by) % length) for i in range(length)])


def layer_body(first, step, agg_own, agg_other, cot_own, cot_other, w, out_own, out_other, grad):
    for at in range(0, grad.shape[0], step):
        src, dst = pl.ds(first + at, step), pl.ds(at, step)
        rows = w[src, :]
        total = None
        for agg, cot, out in ((agg_own, cot_own, out_own), (agg_other, cot_other, out_other)):
            pre = lax.dot_general(rows, agg[...], TURN, preferred_element_type=F32)
            s = jax.nn.sigmoid(pre)
            out[dst, :] = (pre * s).astype(BF16)
            slope = s * (1.0 + pre * (1.0 - s))
            grad_pre = (cot[src, :].astype(F32) * slope).astype(BF16)
            term = jnp.dot(grad_pre, agg[...], preferred_element_type=F32)
            total = term if total is None else total + term
        grad[dst, :] = total.astype(grad.dtype)


def layer(operands, first, count, kind):
    nodes, width = operands[0].shape

    def body(*refs):
        layer_body(first, 128, *refs)

    return pl.pallas_call(
        body,
        out_shape=[
            jax.ShapeDtypeStruct((count, nodes), BF16),
            jax.ShapeDtypeStruct((count, nodes), BF16),
            jax.ShapeDtypeStruct((count, width), kind),
        ],
        in_specs=[IN_VMEM] * 5,
        out_specs=[IN_VMEM] * 3,
        compiler_params=LIMIT,
        cost_estimate=LONG,
        name="layer",
    )(*operands)


def one_hot_rows(me, rows, width):
    slots = width // rows // 2
    owner = jnp.repeat((2 * jnp.arange(slots, dtype=jnp.int32)) ^ me, rows)
    at = owner * rows + jnp.tile(jnp.arange(rows, dtype=jnp.int32), slots)
    return (at[:, None] == jnp.arange(width, dtype=jnp.int32)[None, :]).astype(BF16)


def local_any(features, tiles, tile_cols, tile_count, weight, cotangent):
    total = lax.axis_size(AXES)
    group_len = lax.axis_size("blk")
    position = lax.axis_index("blk")
    me = lax.axis_index(AXES)
    slot_total = tiles.shape[1]
    rows, width = weight.shape
    in_use = jnp.arange(slot_total, dtype=jnp.int32) < tile_count[0]
    columns = tile_cols[0] % group_len

    held = weight
    bit = 2
    while bit < total:
        held = jnp.concatenate([held, swap(held, bit)])
        bit *= 2

    blocks = [(position, features)]
    for offset in range(1, (slot_total - 1) // 2 + 1):
        blocks.append(((position - offset) % group_len, shifted(features, offset)))
        blocks.append(((position + offset) % group_len, shifted(features, -offset)))
    summed = 0.0
    for source, block in blocks:
        match = jnp.logical_and(in_use, columns == source)
        tile = jnp.sum(jnp.where(match[:, None, None], tiles[0], 0), axis=0, dtype=BF16)
        summed = summed + jnp.dot(tile, block, preferred_element_type=F32)
    agg_own = summed.astype(BF16)
    agg_other = swap(agg_own, CORE)

    mine = one_hot_rows(me, rows, width)
    others = one_hot_rows(me ^ CORE, rows, width)
    cot_own = lax.dot_general(mine, cotangent, TURN, preferred_element_type=F32).astype(BF16)
    cot_other = lax.dot_general(others, cotangent, TURN, preferred_element_type=F32).astype(BF16)
    operands = (agg_own, agg_other, cot_own, swap(cot_other, CORE), held)
    out_own, out_other, grad = layer(operands, 0, width // 2, F32)
    bit = total // 2
    while bit > 1:
        n = grad.shape[0] // 2
        grad = grad[:n] + swap(grad[n:].astype(BF16), bit).astype(F32)
        bit //= 2
    out_t = jnp.concatenate([out_own, swap(out_other, CORE)])
    place = jnp.concatenate([mine, others])
    output = lax.dot_general(out_t, place, (((0,), (0,)), ((), ())), preferred_element_type=F32)
    return output.astype(BF16), grad


def hold_body(weight, near_block, out):
    out[...] = weight[...]


def hold(weight, near_block):
    return pl.pallas_call(
        hold_body,
        out_shape=jax.ShapeDtypeStruct(weight.shape, BF16),
        in_specs=[IN_VMEM, pl.BlockSpec(memory_space=pl.ANY)],
        out_specs=IN_VMEM,
        compiler_params=LIMIT,
        cost_estimate=LONG,
        name="hold",
    )(weight, near_block)


def prepare_body(
    me_ref, cols, count, tiles_in, features_in, cotangent_in, near_block,
    partial, tile_x, cot_own, cot_other, place, tiles, features, cotangent, sems,
):
    copies = [
        pltpu.make_async_copy(src, dst, sems.at[k])
        for k, (src, dst) in enumerate(
            ((tiles_in, tiles), (features_in, features), (cotangent_in, cotangent))
        )
    ]
    for copy in copies:
        copy.start()
    me = me_ref[0]
    core = me % 2
    position = me % 4
    width = features.shape[1]
    half = width // 2
    rows = half // 16

    def tile_of(source):
        chosen = jnp.zeros(tiles.shape[2:], BF16)
        for k in range(tiles.shape[1]):
            match = jnp.logical_and(k < count[0], cols[0, k] % 4 == source)
            chosen = jnp.where(match, tiles[0, k], chosen)
        return chosen

    row_at = lax.broadcasted_iota(jnp.int32, (rows, width), 0)
    column_at = lax.broadcasted_iota(jnp.int32, (rows, width), 1)
    for whose in range(2):
        even = core == whose
        first, second = jnp.where(even, X, Y), jnp.where(even, Y, X)
        for slot in range(16):
            mask = (slot // 8) * first + (slot // 4 % 2) * second + ALONG_Z[slot % 4]
            start = (me ^ whose ^ mask) * rows
            at = whose * half + slot * rows
            place[at : at + rows, :] = (column_at == row_at + start).astype(BF16)
    copies[0].wait()
    copies[1].wait()
    tile_x[...] = tile_of(position ^ (X ^ CORE))
    partial[...] = jnp.dot(
        tile_of(position), features[...], preferred_element_type=F32
    ) + jnp.dot(tile_of(position ^ CORE), near_block[...], preferred_element_type=F32)
    copies[2].wait()
    for whose, cot in ((0, cot_own), (1, cot_other)):
        cot[...] = lax.dot_general(
            place[whose * half : (whose + 1) * half, :], cotangent[...], TURN,
            preferred_element_type=F32,
        ).astype(BF16)


def prepare(me, cols, count, tiles, features, cotangent, near_block):
    nodes, width = features.shape
    half = width // 2
    side = tiles.shape[2]
    return pl.pallas_call(
        prepare_body,
        out_shape=[
            jax.ShapeDtypeStruct((nodes, width), F32),
            jax.ShapeDtypeStruct((side, side), BF16),
            jax.ShapeDtypeStruct((half, nodes), BF16),
            jax.ShapeDtypeStruct((half, nodes), BF16),
            jax.ShapeDtypeStruct((width, width), BF16),
        ],
        in_specs=[IN_SMEM] * 3 + [pl.BlockSpec(memory_space=pltpu.HBM)] * 3 + [IN_VMEM],
        out_specs=[IN_VMEM] * 5,
        scratch_shapes=[
            pltpu.VMEM(tiles.shape, BF16),
            pltpu.VMEM(features.shape, BF16),
            pltpu.VMEM(cotangent.shape, BF16),
            pltpu.SemaphoreType.DMA((3,)),
        ],
        compiler_params=LIMIT,
        cost_estimate=BRIEF,
        name="prepare",
    )(me, cols, count, tiles, features, cotangent, near_block)


def aggregate_body(partial, tile, block, out):
    out[...] = (
        partial[...] + jnp.dot(tile[...], block[...], preferred_element_type=F32)
    ).astype(BF16)


def aggreafter(partial, tile, block):
    return pl.pallas_call(
        aggregate_body,
        out_shape=jax.ShapeDtypeStruct(partial.shape, BF16),
        in_specs=[IN_VMEM] * 3,
        out_specs=IN_VMEM,
        compiler_params=LIMIT,
        cost_estimate=LONG,
        name="aggregate",
    )(partial, tile, block)


def order_body(me_ref, *refs):
    pieces, w = refs[:8], refs[8]
    rows = pieces[0].shape[0] // 2
    even = me_ref[0] % 2 == 0
    for first in range(2):
        for second in range(2):
            for z in range(4):
                by_x = pieces[second * 4 + z][first * rows : (first + 1) * rows, :]
                by_y = pieces[first * 4 + z][second * rows : (second + 1) * rows, :]
                at = ((first * 2 + second) * 4 + z) * rows
                w[at : at + rows, :] = jnp.where(even, by_x, by_y)


def into_place_body(*refs):
    parts, place, out = refs[:-2], refs[-2], refs[-1]
    at, total = 0, 0.0
    for part in parts:
        count = part.shape[0]
        total += lax.dot_general(
            part[...], place[at : at + count, :], (((0,), (0,)), ((), ())),
            preferred_element_type=F32,
        )
        at += count
    out[...] = total.astype(out.dtype)


def into_place(parts, place):
    return pl.pallas_call(
        into_place_body,
        out_shape=jax.ShapeDtypeStruct((parts[0].shape[1], place.shape[1]), BF16),
        in_specs=[IN_VMEM] * (len(parts) + 1),
        out_specs=IN_VMEM,
        compiler_params=LIMIT,
        cost_estimate=BRIEF,
        name="into_place",
    )(*parts, place)


def add(kept, first, count, got, kind, cost=BRIEF):
    def body(kept_ref, got_ref, out):
        out[...] = (kept_ref[pl.ds(first, count), :] + got_ref[...].astype(F32)).astype(kind)

    return pl.pallas_call(
        body,
        out_shape=jax.ShapeDtypeStruct((count, kept.shape[1]), kind),
        in_specs=[IN_VMEM] * 2,
        out_specs=IN_VMEM,
        compiler_params=LIMIT,
        cost_estimate=cost,
        name="add",
    )(kept, got)


def in_order(me, pieces):
    rows, width = pieces[0].shape
    return pl.pallas_call(
        order_body,
        out_shape=jax.ShapeDtypeStruct((8 * rows, width), BF16),
        in_specs=[IN_SMEM] + [IN_VMEM] * 8,
        out_specs=IN_VMEM,
        compiler_params=LIMIT,
        cost_estimate=LONG,
        name="in_order",
    )(me, *pieces)


def local_cube(features, tiles, tile_cols, tile_count, weight, cotangent):
    me = lax.axis_index(AXES).astype(jnp.int32).reshape(1)
    rows, width = weight.shape

    near_block = swap(features, CORE)
    weight_x = swap(weight, X)
    x_block = swap(after(features, near_block), X ^ CORE)
    pair = jnp.concatenate([hold(weight, near_block), weight_x])
    far = swap(pair, FAR)
    near = swap(pair, NEAR)
    pieces = {(0, 0): pair, (0, NEAR): near}
    pieces[1, 0] = swap(pair, Y)
    pieces[1, NEAR] = swap(pair, Y ^ NEAR)
    partial, tile_x, cot_own, cot_other, place = prepare(
        after(me, pair), tile_cols, tile_count, tiles, features, cotangent, near_block
    )
    cot_other = swap(cot_other, CORE)
    far = after(far, near, pieces[1, 0])
    pieces[0, FAR] = far
    pieces[1, FAR] = swap(far, Y)
    pieces[0, NEAR ^ FAR] = swap(far, NEAR)
    pieces[1, NEAR ^ FAR] = swap(far, Y ^ NEAR)

    agg_own = aggreafter(partial, tile_x, x_block)
    agg_other = swap(agg_own, CORE)
    w = in_order(me, [pieces[y, z] for y in range(2) for z in ALONG_Z])
    operands = (agg_own, agg_other, cot_own, cot_other, w)

    quarter = width // 8
    own_3, other_3, grad_3 = layer(operands, 3 * quarter, quarter, BF16)
    got_3 = swap(grad_3, X, Y)
    own_2, other_2, grad_2 = layer(operands, 2 * quarter, quarter, BF16)
    got_2 = swap(grad_2, X, Y)
    own_1, other_1, keep = layer(operands, 0, 2 * quarter, F32)

    from_other = swap(jnp.concatenate([other_1, other_2, other_3]), CORE)
    output = into_place([own_1, own_2, own_3, from_other], place)

    send_hi = add(keep, quarter + 2 * rows, 2 * rows, got_3[2 * rows :], BF16)
    got_hi = swap(send_hi, Y, X)
    send_lo = add(keep, quarter, 2 * rows, got_3[: 2 * rows], BF16)
    got_lo = swap(send_lo, Y, X)
    got_hi = after(got_hi, output)
    keep = add(keep, 0, quarter, got_2, F32, LONG)
    high_16 = add(keep, 3 * rows, rows, got_hi[rows:], BF16)
    got_16 = swap(high_16, ALONG_Z[3])
    high_24 = add(keep, 2 * rows, rows, got_hi[:rows], BF16)
    got_24 = swap(high_24, ALONG_Z[2])
    got_lo = after(got_lo, high_24, high_16)
    got_8 = swap(add(keep, rows, rows, got_lo[rows:], BF16, LONG), ALONG_Z[1])
    mine = keep[:rows] + got_lo[:rows].astype(F32)
    return output, mine + sum(v.astype(F32) for v in (got_24, got_16, got_8))


def solution(mesh):
    cube = mesh.shape["rows"] == 8 and mesh.shape["blk"] == 4
    in_specs = (
        P(AXES, None),
        P(AXES, None, None, None),
        P(AXES, None),
        P(AXES),
        P(AXES, None),
        P(AXES, None),
    )
    out_specs = (P(AXES, None), P(AXES, None))
    return jax.shard_map(
        local_cube if cube else local_any,
        mesh=mesh,
        in_specs=in_specs,
        out_specs=out_specs,
        check_vma=False,
    )
```

```python
import jax
import jax.numpy as jnp
from jax import lax
from jax.experimental import pallas as pl
from jax.experimental.pallas import tpu as pltpu
from jax.sharding import PartitionSpec as P

AXES = ("rows", "blk")
CORE, X, Y, NEAR, FAR = 1, 2, 4, 8, 16
ALONG_Z = (0, NEAR, NEAR ^ FAR, FAR)
F32 = jnp.float32
BF16 = jnp.bfloat16
TURN = (((1,), (1,)), ((), ()))
IN_VMEM = pl.BlockSpec(memory_space=pltpu.VMEM)
IN_SMEM = pl.BlockSpec(memory_space=pltpu.SMEM)
LIMIT = pltpu.CompilerParams(vmem_limit_bytes=24 * 1024 * 1024)
BRIEF = pl.CostEstimate(flops=0, bytes_accessed=0, transcendentals=0)
LONG = pl.CostEstimate(flops=20_000_000_000, bytes_accessed=0, transcendentals=0)


def swap(value, mask, odd_mask=None):
    total = lax.axis_size(AXES)
    masks = (mask, mask if odd_mask is None else odd_mask)
    return lax.ppermute(value, AXES, [(i, i ^ masks[i % 2]) for i in range(total)])


def after(value, *earlier):
    return lax.optimization_barrier((value, *earlier))[0]


def shifted(value, by):
    length = lax.axis_size("blk")
    return lax.ppermute(value, "blk", [(i, (i + by) % length) for i in range(length)])


def layer_body(first, cot_first, step, agg_own, agg_other, cot_own, cot_other, w, out_own, out_other, grad):
    for at in range(0, grad.shape[0], step):
        dst = pl.ds(at, step)
        rows = w[pl.ds(first + at, step), :]
        total = None
        for agg, cot, out in ((agg_own, cot_own, out_own), (agg_other, cot_other, out_other)):
            pre = lax.dot_general(rows, agg[...], TURN, preferred_element_type=F32)
            s = jax.nn.sigmoid(pre)
            out[dst, :] = (pre * s).astype(BF16)
            slope = s * (1.0 + pre * (1.0 - s))
            grad_pre = (cot[pl.ds(cot_first + at, step), :].astype(F32) * slope).astype(BF16)
            term = jnp.dot(grad_pre, agg[...], preferred_element_type=F32)
            total = term if total is None else total + term
        grad[dst, :] = total.astype(grad.dtype)


def layer(operands, first, cot_first, count, kind):
    nodes, width = operands[0].shape

    def body(*refs):
        layer_body(first, cot_first, 128, *refs)

    return pl.pallas_call(
        body,
        out_shape=[
            jax.ShapeDtypeStruct((count, nodes), BF16),
            jax.ShapeDtypeStruct((count, nodes), BF16),
            jax.ShapeDtypeStruct((count, width), kind),
        ],
        in_specs=[IN_VMEM] * 5,
        out_specs=[IN_VMEM] * 3,
        compiler_params=LIMIT,
        cost_estimate=LONG,
        name="layer",
    )(*operands)


def one_hot_rows(me, rows, width):
    slots = width // rows // 2
    owner = jnp.repeat((2 * jnp.arange(slots, dtype=jnp.int32)) ^ me, rows)
    at = owner * rows + jnp.tile(jnp.arange(rows, dtype=jnp.int32), slots)
    return (at[:, None] == jnp.arange(width, dtype=jnp.int32)[None, :]).astype(BF16)


def local_any(features, tiles, tile_cols, tile_count, weight, cotangent):
    total = lax.axis_size(AXES)
    group_len = lax.axis_size("blk")
    position = lax.axis_index("blk")
    me = lax.axis_index(AXES)
    slot_total = tiles.shape[1]
    rows, width = weight.shape
    in_use = jnp.arange(slot_total, dtype=jnp.int32) < tile_count[0]
    columns = tile_cols[0] % group_len

    held = weight
    bit = 2
    while bit < total:
        held = jnp.concatenate([held, swap(held, bit)])
        bit *= 2

    blocks = [(position, features)]
    for offset in range(1, (slot_total - 1) // 2 + 1):
        blocks.append(((position - offset) % group_len, shifted(features, offset)))
        blocks.append(((position + offset) % group_len, shifted(features, -offset)))
    summed = 0.0
    for source, block in blocks:
        match = jnp.logical_and(in_use, columns == source)
        tile = jnp.sum(jnp.where(match[:, None, None], tiles[0], 0), axis=0, dtype=BF16)
        summed = summed + jnp.dot(tile, block, preferred_element_type=F32)
    agg_own = summed.astype(BF16)
    agg_other = swap(agg_own, CORE)

    mine = one_hot_rows(me, rows, width)
    others = one_hot_rows(me ^ CORE, rows, width)
    cot_own = lax.dot_general(mine, cotangent, TURN, preferred_element_type=F32).astype(BF16)
    cot_other = lax.dot_general(others, cotangent, TURN, preferred_element_type=F32).astype(BF16)
    operands = (agg_own, agg_other, cot_own, swap(cot_other, CORE), held)
    out_own, out_other, grad = layer(operands, 0, 0, width // 2, F32)
    bit = total // 2
    while bit > 1:
        n = grad.shape[0] // 2
        grad = grad[:n] + swap(grad[n:].astype(BF16), bit).astype(F32)
        bit //= 2
    out_t = jnp.concatenate([out_own, swap(out_other, CORE)])
    place = jnp.concatenate([mine, others])
    output = lax.dot_general(out_t, place, (((0,), (0,)), ((), ())), preferred_element_type=F32)
    return output.astype(BF16), grad


def hold_body(weight, near_block, out):
    out[...] = weight[...]


def hold(weight, near_block):
    return pl.pallas_call(
        hold_body,
        out_shape=jax.ShapeDtypeStruct(weight.shape, BF16),
        in_specs=[IN_VMEM, pl.BlockSpec(memory_space=pl.ANY)],
        out_specs=IN_VMEM,
        compiler_params=LIMIT,
        cost_estimate=LONG,
        name="hold",
    )(weight, near_block)


def prepare_body(
    me_ref, cols, count, tiles_in, features_in, cotangent_in, near_block,
    partial, tile_x, cot_own, cot_other, place, tiles, features, cotangent, sems,
):
    copies = [
        pltpu.make_async_copy(src, dst, sems.at[k])
        for k, (src, dst) in enumerate(
            ((tiles_in, tiles), (features_in, features), (cotangent_in, cotangent))
        )
    ]
    for copy in copies:
        copy.start()
    me = me_ref[0]
    core = me % 2
    position = me % 4
    width = features.shape[1]
    half = width // 2
    rows = half // 16

    def tile_of(source):
        chosen = jnp.zeros(tiles.shape[2:], BF16)
        for k in range(tiles.shape[1]):
            match = jnp.logical_and(k < count[0], cols[0, k] % 4 == source)
            chosen = jnp.where(match, tiles[0, k], chosen)
        return chosen

    row_at = lax.broadcasted_iota(jnp.int32, (rows, width), 0)
    column_at = lax.broadcasted_iota(jnp.int32, (rows, width), 1)
    for whose in range(2):
        even = core == whose
        first, second = jnp.where(even, X, Y), jnp.where(even, Y, X)
        for slot in range(16):
            z = ALONG_Z[slot // 8 * 2 + slot % 2]
            mask = (slot // 4 % 2) * first + (slot // 2 % 2) * second + z
            start = (me ^ whose ^ mask) * rows
            at = whose * half + slot * rows
            place[at : at + rows, :] = (column_at == row_at + start).astype(BF16)
    copies[0].wait()
    copies[1].wait()
    tile_x[...] = tile_of(position ^ (X ^ CORE))
    partial[...] = jnp.dot(
        tile_of(position), features[...], preferred_element_type=F32
    ) + jnp.dot(tile_of(position ^ CORE), near_block[...], preferred_element_type=F32)
    copies[2].wait()
    for whose, cot in ((0, cot_own), (1, cot_other)):
        cot[...] = lax.dot_general(
            place[whose * half : (whose + 1) * half, :], cotangent[...], TURN,
            preferred_element_type=F32,
        ).astype(BF16)


def prepare(me, cols, count, tiles, features, cotangent, near_block):
    nodes, width = features.shape
    half = width // 2
    side = tiles.shape[2]
    return pl.pallas_call(
        prepare_body,
        out_shape=[
            jax.ShapeDtypeStruct((nodes, width), F32),
            jax.ShapeDtypeStruct((side, side), BF16),
            jax.ShapeDtypeStruct((half, nodes), BF16),
            jax.ShapeDtypeStruct((half, nodes), BF16),
            jax.ShapeDtypeStruct((width, width), BF16),
        ],
        in_specs=[IN_SMEM] * 3 + [pl.BlockSpec(memory_space=pltpu.HBM)] * 3 + [IN_VMEM],
        out_specs=[IN_VMEM] * 5,
        scratch_shapes=[
            pltpu.VMEM(tiles.shape, BF16),
            pltpu.VMEM(features.shape, BF16),
            pltpu.VMEM(cotangent.shape, BF16),
            pltpu.SemaphoreType.DMA((3,)),
        ],
        compiler_params=LIMIT,
        cost_estimate=BRIEF,
        name="prepare",
    )(me, cols, count, tiles, features, cotangent, near_block)


def aggregate_body(partial, tile, block, out):
    out[...] = (
        partial[...] + jnp.dot(tile[...], block[...], preferred_element_type=F32)
    ).astype(BF16)


def aggregate(partial, tile, block):
    return pl.pallas_call(
        aggregate_body,
        out_shape=jax.ShapeDtypeStruct(partial.shape, BF16),
        in_specs=[IN_VMEM] * 3,
        out_specs=IN_VMEM,
        compiler_params=LIMIT,
        cost_estimate=BRIEF,
        name="aggregate",
    )(partial, tile, block)


def order_body(me_ref, *refs):
    pieces, w = refs[:4], refs[4]
    rows = pieces[0].shape[0] // 2
    even = me_ref[0] % 2 == 0
    for first in range(2):
        for second in range(2):
            for z in range(2):
                by_x = pieces[second * 2 + z][first * rows : (first + 1) * rows, :]
                by_y = pieces[first * 2 + z][second * rows : (second + 1) * rows, :]
                at = ((first * 2 + second) * 2 + z) * rows
                w[at : at + rows, :] = jnp.where(even, by_x, by_y)


def in_order(me, pieces):
    rows, width = pieces[0].shape
    return pl.pallas_call(
        order_body,
        out_shape=jax.ShapeDtypeStruct((4 * rows, width), BF16),
        in_specs=[IN_SMEM] + [IN_VMEM] * 4,
        out_specs=IN_VMEM,
        compiler_params=LIMIT,
        cost_estimate=LONG,
        name="in_order",
    )(me, *pieces)


def into_place_body(*refs):
    parts, place, out = refs[:-2], refs[-2], refs[-1]
    at, total = 0, 0.0
    for part in parts:
        count = part.shape[0]
        total += lax.dot_general(
            part[...], place[at : at + count, :], (((0,), (0,)), ((), ())),
            preferred_element_type=F32,
        )
        at += count
    out[...] = total.astype(out.dtype)


def into_place(parts, place):
    return pl.pallas_call(
        into_place_body,
        out_shape=jax.ShapeDtypeStruct((parts[0].shape[1], place.shape[1]), BF16),
        in_specs=[IN_VMEM] * (len(parts) + 1),
        out_specs=IN_VMEM,
        compiler_params=LIMIT,
        cost_estimate=BRIEF,
        name="into_place",
    )(*parts, place)


def add(kept, first, count, got, kind, cost=BRIEF):
    def body(kept_ref, got_ref, out):
        out[...] = (kept_ref[pl.ds(first, count), :] + got_ref[...].astype(F32)).astype(kind)

    return pl.pallas_call(
        body,
        out_shape=jax.ShapeDtypeStruct((count, kept.shape[1]), kind),
        in_specs=[IN_VMEM] * 2,
        out_specs=IN_VMEM,
        compiler_params=LIMIT,
        cost_estimate=cost,
        name="add",
    )(kept, got)


def local_cube(features, tiles, tile_cols, tile_count, weight, cotangent):
    me = lax.axis_index(AXES).astype(jnp.int32).reshape(1)
    rows, width = weight.shape

    near_block = swap(features, CORE)
    weight_x = swap(weight, X)
    x_block = swap(after(features, near_block), X ^ CORE)
    pair = jnp.concatenate([hold(weight, near_block), weight_x])
    far = swap(pair, FAR)
    near = swap(pair, NEAR)
    pieces = {(0, 0): pair, (0, NEAR): near}
    pieces[1, 0] = swap(pair, Y)
    pieces[1, NEAR] = swap(pair, Y ^ NEAR)
    partial, tile_x, cot_own, cot_other, place = prepare(
        after(me, pair), tile_cols, tile_count, tiles, features, cotangent, near_block
    )
    cot_other = swap(after(cot_other, x_block), CORE)
    far = after(far, near, pieces[1, 0])
    pieces[0, FAR] = far
    pieces[1, FAR] = swap(far, Y)
    pieces[0, NEAR ^ FAR] = swap(far, NEAR)
    pieces[1, NEAR ^ FAR] = swap(far, Y ^ NEAR)

    agg_own = aggregate(partial, tile_x, x_block)
    agg_other = swap(agg_own, CORE)
    order_e = [pieces[y, z] for y in range(2) for z in ALONG_Z[:2]]
    order_e[0] = after(order_e[0], agg_own)
    w_e = in_order(me, order_e)
    operands = [agg_own, agg_other, cot_own, cot_other]
    own_e1, other_e1, send_e = layer(operands + [w_e], 4 * rows, 4 * rows, 4 * rows, BF16)
    got_e = swap(send_e, X, Y)
    order_l = [pieces[y, z] for y in range(2) for z in ALONG_Z[2:]]
    order_l[0] = after(order_l[0], send_e)
    w_l = in_order(me, order_l)
    own_l1, other_l1, send_l = layer(operands + [w_l], 4 * rows, 12 * rows, 4 * rows, BF16)
    got_l = swap(send_l, X, Y)
    w_e = after(w_e, send_l)
    own_e0, other_e0, keep_e = layer(operands + [w_e], 0, 0, 4 * rows, F32)
    own_l0, other_l0, keep_l = layer(operands + [w_l], 0, 8 * rows, 4 * rows, F32)

    sums = []
    for got, keep in ((got_e, keep_e), (got_l, keep_l)):
        send = add(keep, 2 * rows, 2 * rows, got[2 * rows :], BF16)
        sums.append((swap(send, Y, X), add(keep, 0, 2 * rows, got[: 2 * rows], F32)))

    others = jnp.concatenate([other_e0, other_e1, other_l0, other_l1])
    from_other = swap(others, CORE)
    output = into_place([own_e0, own_e1, own_l0, own_l1, from_other], place)

    (got_e, keep_e), (got_l, keep_l) = sums
    got_8 = swap(add(keep_e, rows, rows, got_e[rows:], BF16), ALONG_Z[1])
    got_l = after(got_l, output)
    got_16 = swap(add(keep_l, rows, rows, got_l[rows:], BF16), ALONG_Z[3])
    got_24 = swap(add(keep_l, 0, rows, got_l[:rows], BF16), ALONG_Z[2])
    mine = keep_e[:rows] + got_e[:rows].astype(F32)
    return output, mine + sum(v.astype(F32) for v in (got_24, got_16, got_8))


def solution(mesh):
    cube = mesh.shape["rows"] == 8 and mesh.shape["blk"] == 4
    in_specs = (
        P(AXES, None),
        P(AXES, None, None, None),
        P(AXES, None),
        P(AXES),
        P(AXES, None),
        P(AXES, None),
    )
    out_specs = (P(AXES, None), P(AXES, None))
    return jax.shard_map(
        local_cube if cube else local_any,
        mesh=mesh,
        in_specs=in_specs,
        out_specs=out_specs,
        check_vma=False,
    )
```

```python
import jax
import jax.numpy as jnp
from jax import lax
from jax.experimental import pallas as pl
from jax.experimental.pallas import tpu as pltpu
from jax.sharding import PartitionSpec as P

AXES = ("rows", "blk")
CORE, X, Y, NEAR, FAR = 1, 2, 4, 8, 16
ALONG_Z = (0, NEAR, NEAR ^ FAR, FAR)
F32 = jnp.float32
BF16 = jnp.bfloat16
TURN = (((1,), (1,)), ((), ()))
IN_VMEM = pl.BlockSpec(memory_space=pltpu.VMEM)
IN_SMEM = pl.BlockSpec(memory_space=pltpu.SMEM)
LIMIT = pltpu.CompilerParams(vmem_limit_bytes=24 * 1024 * 1024)
BRIEF = pl.CostEstimate(flops=0, bytes_accessed=0, transcendentals=0)
LONG = pl.CostEstimate(flops=20_000_000_000, bytes_accessed=0, transcendentals=0)


def swap(value, mask, odd_mask=None):
    total = lax.axis_size(AXES)
    masks = (mask, mask if odd_mask is None else odd_mask)
    return lax.ppermute(value, AXES, [(i, i ^ masks[i % 2]) for i in range(total)])


def after(value, *earlier):
    return lax.optimization_barrier((value, *earlier))[0]


def shifted(value, by):
    length = lax.axis_size("blk")
    return lax.ppermute(value, "blk", [(i, (i + by) % length) for i in range(length)])


def layer_rows(operands, first, cot_first, step, outs, at):
    w = operands[4]
    rows, dst = w[pl.ds(first, step), :], pl.ds(at, step)
    total = None
    for agg, cot, out in zip(operands[:2], operands[2:4], outs):
        pre = lax.dot_general(rows, agg[...], TURN, preferred_element_type=F32)
        s = jax.nn.sigmoid(pre)
        out[dst, :] = (pre * s).astype(BF16)
        slope = s * (1.0 + pre * (1.0 - s))
        grad_pre = (cot[pl.ds(cot_first, step), :].astype(F32) * slope).astype(BF16)
        term = jnp.dot(grad_pre, agg[...], preferred_element_type=F32)
        total = term if total is None else total + term
    return total


def layer(operands, first, cot_first, count, kinds, cost=LONG):
    nodes, width = operands[0].shape
    part = count // len(kinds)
    step = min(128, count)

    def body(*refs):
        operands, outs, grads = refs[:5], refs[5:7], refs[7:]
        for at in range(0, count, step):
            total = layer_rows(operands, first + at, cot_first + at, step, outs, at)
            for k, grad in enumerate(grads):
                if len(grads) == 1:
                    grad[pl.ds(at, step), :] = total.astype(grad.dtype)
                else:
                    grad[...] = total[k * part : (k + 1) * part, :].astype(grad.dtype)

    assert len(kinds) == 1 or count == step
    return pl.pallas_call(
        body,
        out_shape=[jax.ShapeDtypeStruct((count, nodes), BF16)] * 2
        + [jax.ShapeDtypeStruct((part, width), kind) for kind in kinds],
        in_specs=[IN_VMEM] * 5,
        out_specs=[IN_VMEM] * (2 + len(kinds)),
        compiler_params=LIMIT,
        cost_estimate=cost,
        name="layer",
    )(*operands)


def one_hot_rows(me, rows, width):
    slots = width // rows // 2
    owner = jnp.repeat((2 * jnp.arange(slots, dtype=jnp.int32)) ^ me, rows)
    at = owner * rows + jnp.tile(jnp.arange(rows, dtype=jnp.int32), slots)
    return (at[:, None] == jnp.arange(width, dtype=jnp.int32)[None, :]).astype(BF16)


def local_any(features, tiles, tile_cols, tile_count, weight, cotangent):
    total = lax.axis_size(AXES)
    group_len = lax.axis_size("blk")
    position = lax.axis_index("blk")
    me = lax.axis_index(AXES)
    slot_total = tiles.shape[1]
    rows, width = weight.shape
    in_use = jnp.arange(slot_total, dtype=jnp.int32) < tile_count[0]
    columns = tile_cols[0] % group_len

    held = weight
    bit = 2
    while bit < total:
        held = jnp.concatenate([held, swap(held, bit)])
        bit *= 2

    blocks = [(position, features)]
    for offset in range(1, (slot_total - 1) // 2 + 1):
        blocks.append(((position - offset) % group_len, shifted(features, offset)))
        blocks.append(((position + offset) % group_len, shifted(features, -offset)))
    summed = 0.0
    for source, block in blocks:
        match = jnp.logical_and(in_use, columns == source)
        tile = jnp.sum(jnp.where(match[:, None, None], tiles[0], 0), axis=0, dtype=BF16)
        summed = summed + jnp.dot(tile, block, preferred_element_type=F32)
    agg_own = summed.astype(BF16)
    agg_other = swap(agg_own, CORE)

    mine = one_hot_rows(me, rows, width)
    others = one_hot_rows(me ^ CORE, rows, width)
    cot_own = lax.dot_general(mine, cotangent, TURN, preferred_element_type=F32).astype(BF16)
    cot_other = lax.dot_general(others, cotangent, TURN, preferred_element_type=F32).astype(BF16)
    operands = (agg_own, agg_other, cot_own, swap(cot_other, CORE), held)
    out_own, out_other, grad = layer(operands, 0, 0, width // 2, [F32])
    bit = total // 2
    while bit > 1:
        n = grad.shape[0] // 2
        grad = grad[:n] + swap(grad[n:].astype(BF16), bit).astype(F32)
        bit //= 2
    out_t = jnp.concatenate([out_own, swap(out_other, CORE)])
    place = jnp.concatenate([mine, others])
    output = lax.dot_general(out_t, place, (((0,), (0,)), ((), ())), preferred_element_type=F32)
    return output.astype(BF16), grad


def hold_body(weight, near_block, out):
    out[...] = weight[...]


def hold(weight, near_block):
    return pl.pallas_call(
        hold_body,
        out_shape=jax.ShapeDtypeStruct(weight.shape, BF16),
        in_specs=[IN_VMEM, pl.BlockSpec(memory_space=pl.ANY)],
        out_specs=IN_VMEM,
        compiler_params=LIMIT,
        cost_estimate=LONG,
        name="hold",
    )(weight, near_block)


def prepare_body(
    me_ref, cols, count, tiles_in, features_in, cotangent_in, near_block,
    partial, tile_x, cot_own, cot_other, place, tiles, features, cotangent, sems,
):
    copies = [
        pltpu.make_async_copy(src, dst, sems.at[k])
        for k, (src, dst) in enumerate(
            ((tiles_in, tiles), (features_in, features), (cotangent_in, cotangent))
        )
    ]
    for copy in copies:
        copy.start()
    me = me_ref[0]
    core = me % 2
    position = me % 4
    width = features.shape[1]
    half = width // 2
    rows = half // 16

    def tile_of(source):
        chosen = jnp.zeros(tiles.shape[2:], BF16)
        for k in range(tiles.shape[1]):
            match = jnp.logical_and(k < count[0], cols[0, k] % 4 == source)
            chosen = jnp.where(match, tiles[0, k], chosen)
        return chosen

    row_at = lax.broadcasted_iota(jnp.int32, (rows, width), 0)
    column_at = lax.broadcasted_iota(jnp.int32, (rows, width), 1)
    for whose in range(2):
        even = core == whose
        first, second = jnp.where(even, X, Y), jnp.where(even, Y, X)
        for slot in range(16):
            z = ALONG_Z[slot // 8 * 2 + slot % 2]
            mask = (slot // 4 % 2) * first + (slot // 2 % 2) * second + z
            start = (me ^ whose ^ mask) * rows
            at = whose * half + slot * rows
            place[at : at + rows, :] = (column_at == row_at + start).astype(BF16)
    copies[0].wait()
    copies[1].wait()
    tile_x[...] = tile_of(position ^ (X ^ CORE))
    partial[...] = jnp.dot(
        tile_of(position), features[...], preferred_element_type=F32
    ) + jnp.dot(tile_of(position ^ CORE), near_block[...], preferred_element_type=F32)
    copies[2].wait()
    for whose, cot in ((0, cot_own), (1, cot_other)):
        cot[...] = lax.dot_general(
            place[whose * half : (whose + 1) * half, :], cotangent[...], TURN,
            preferred_element_type=F32,
        ).astype(BF16)


def prepare(me, cols, count, tiles, features, cotangent, near_block):
    nodes, width = features.shape
    half = width // 2
    side = tiles.shape[2]
    return pl.pallas_call(
        prepare_body,
        out_shape=[
            jax.ShapeDtypeStruct((nodes, width), F32),
            jax.ShapeDtypeStruct((side, side), BF16),
            jax.ShapeDtypeStruct((half, nodes), BF16),
            jax.ShapeDtypeStruct((half, nodes), BF16),
            jax.ShapeDtypeStruct((width, width), BF16),
        ],
        in_specs=[IN_SMEM] * 3 + [pl.BlockSpec(memory_space=pltpu.HBM)] * 3 + [IN_VMEM],
        out_specs=[IN_VMEM] * 5,
        scratch_shapes=[
            pltpu.VMEM(tiles.shape, BF16),
            pltpu.VMEM(features.shape, BF16),
            pltpu.VMEM(cotangent.shape, BF16),
            pltpu.SemaphoreType.DMA((3,)),
        ],
        compiler_params=LIMIT,
        cost_estimate=BRIEF,
        name="prepare",
    )(me, cols, count, tiles, features, cotangent, near_block)


def aggregate_body(partial, tile, block, out):
    out[...] = (
        partial[...] + jnp.dot(tile[...], block[...], preferred_element_type=F32)
    ).astype(BF16)


def aggregate(partial, tile, block):
    return pl.pallas_call(
        aggregate_body,
        out_shape=jax.ShapeDtypeStruct(partial.shape, BF16),
        in_specs=[IN_VMEM] * 3,
        out_specs=IN_VMEM,
        compiler_params=LIMIT,
        cost_estimate=BRIEF,
        name="aggregate",
    )(partial, tile, block)


def order_body(me_ref, *refs):
    pieces, w = refs[:4], refs[4]
    rows = pieces[0].shape[0] // 2
    even = me_ref[0] % 2 == 0
    for first in range(2):
        for second in range(2):
            for z in range(2):
                by_x = pieces[second * 2 + z][first * rows : (first + 1) * rows, :]
                by_y = pieces[first * 2 + z][second * rows : (second + 1) * rows, :]
                at = ((first * 2 + second) * 2 + z) * rows
                w[at : at + rows, :] = jnp.where(even, by_x, by_y)


def in_order(me, pieces):
    rows, width = pieces[0].shape
    return pl.pallas_call(
        order_body,
        out_shape=jax.ShapeDtypeStruct((4 * rows, width), BF16),
        in_specs=[IN_SMEM] + [IN_VMEM] * 4,
        out_specs=IN_VMEM,
        compiler_params=LIMIT,
        cost_estimate=LONG,
        name="in_order",
    )(me, *pieces)


def into_place_body(*refs):
    parts, place, out = refs[:-2], refs[-2], refs[-1]
    at, total = 0, 0.0
    for part in parts:
        count = part.shape[0]
        total += lax.dot_general(
            part[...], place[at : at + count, :], (((0,), (0,)), ((), ())),
            preferred_element_type=F32,
        )
        at += count
    out[...] = total.astype(out.dtype)


def into_place(parts, place):
    return pl.pallas_call(
        into_place_body,
        out_shape=jax.ShapeDtypeStruct((parts[0].shape[1], place.shape[1]), BF16),
        in_specs=[IN_VMEM] * (len(parts) + 1),
        out_specs=IN_VMEM,
        compiler_params=LIMIT,
        cost_estimate=BRIEF,
        name="into_place",
    )(*parts, place)


def add(kept, first, count, got, kind, cost=BRIEF):
    def body(kept_ref, got_ref, out):
        out[...] = (kept_ref[pl.ds(first, count), :] + got_ref[...].astype(F32)).astype(kind)

    return pl.pallas_call(
        body,
        out_shape=jax.ShapeDtypeStruct((count, kept.shape[1]), kind),
        in_specs=[IN_VMEM] * 2,
        out_specs=IN_VMEM,
        compiler_params=LIMIT,
        cost_estimate=cost,
        name="add",
    )(kept, got)


def local_cube(features, tiles, tile_cols, tile_count, weight, cotangent):
    me = lax.axis_index(AXES).astype(jnp.int32).reshape(1)
    rows, width = weight.shape

    weight_x = swap(weight, X)
    tick = swap(tile_count, CORE)
    x_block = swap(after(features, tick), X ^ CORE)
    pair = jnp.concatenate([hold(weight, tick), weight_x])
    near_block = swap(after(features, tick), CORE)
    far = swap(pair, FAR)
    near = swap(pair, NEAR)
    pieces = {(0, 0): pair, (0, NEAR): near}
    pieces[1, 0] = swap(pair, Y)
    pieces[1, NEAR] = swap(pair, Y ^ NEAR)
    partial, tile_x, cot_own, cot_other, place = prepare(
        after(me, pair), tile_cols, tile_count, tiles, features, cotangent, near_block
    )
    cot_other = swap(after(cot_other, x_block), CORE)
    far = after(far, pieces[1, 0], partial)
    pieces[0, FAR] = far
    pieces[1, FAR] = swap(far, Y)
    pieces[1, NEAR ^ FAR] = swap(far, Y ^ NEAR)

    agg_own = aggregate(partial, tile_x, x_block)
    agg_other = swap(agg_own, CORE)
    pieces[0, NEAR ^ FAR] = swap(after(far, agg_own), NEAR)
    order_e = [pieces[y, z] for y in range(2) for z in ALONG_Z[:2]]
    order_e[0] = after(order_e[0], agg_own)
    w_e = in_order(me, order_e)
    operands = [agg_own, agg_other, cot_own, cot_other]
    half = 2 * rows
    own_e1, other_e1, send_e = layer(operands + [w_e], 2 * half, 2 * half, 2 * half, [BF16])
    got_e = swap(send_e, X, Y)
    order_l = [pieces[y, z] for y in range(2) for z in ALONG_Z[2:]]
    order_l[0] = after(order_l[0], send_e)
    w_l = in_order(me, order_l)
    own_l1, other_l1, send_0, send_1 = layer(
        operands + [w_l], 2 * half, 6 * half, 2 * half, [BF16] * 2
    )
    got_1 = swap(send_1, X, Y)
    got_0 = swap(send_0, X, Y)
    w_e = after(w_e, send_1)
    own_e0, other_e0, keep_e = layer(operands + [w_e], 0, 0, 2 * half, [F32])
    own_l0, other_l0, keep_l = layer(operands + [w_l], 0, 4 * half, 2 * half, [F32])

    send = add(keep_e, half, half, got_e[half:], BF16)
    keep_e = add(keep_e, 0, half, got_e[:half], F32)
    got_e = swap(send, Y, X)

    got_24 = swap(add(keep_l, half, rows, got_1[:rows], BF16), Y, X)
    got_16 = swap(add(keep_l, half + rows, rows, got_1[rows:], BF16), Y, X)
    keep_l = add(keep_l, 0, half, got_0, F32)

    others = jnp.concatenate([other_e0, other_e1, other_l0, other_l1])
    from_other = swap(others, CORE)
    output = into_place([own_e0, own_e1, own_l0, own_l1, from_other], place)

    got_8 = swap(add(keep_e, rows, rows, got_e[rows:], BF16), ALONG_Z[1])
    got_24, got_16 = after(got_24, output), after(got_16, output)
    got_24 = swap(add(keep_l, 0, rows, got_24, BF16), ALONG_Z[2])
    got_16 = swap(add(keep_l, rows, rows, got_16, BF16), ALONG_Z[3])
    mine = keep_e[:rows] + got_e[:rows].astype(F32)
    return output, mine + sum(v.astype(F32) for v in (got_24, got_16, got_8))


def solution(mesh):
    cube = mesh.shape["rows"] == 8 and mesh.shape["blk"] == 4
    in_specs = (
        P(AXES, None),
        P(AXES, None, None, None),
        P(AXES, None),
        P(AXES),
        P(AXES, None),
        P(AXES, None),
    )
    out_specs = (P(AXES, None), P(AXES, None))
    return jax.shard_map(
        local_cube if cube else local_any,
        mesh=mesh,
        in_specs=in_specs,
        out_specs=out_specs,
        check_vma=False,
    )
```

```python
import jax
import jax.numpy as jnp
from jax import lax
from jax.experimental import pallas as pl
from jax.experimental.pallas import tpu as pltpu
from jax.sharding import PartitionSpec as P

AXES = ("rows", "blk")
CORE, X, Y, NEAR, FAR = 1, 2, 4, 8, 16
ALONG_Z = (0, NEAR, NEAR ^ FAR, FAR)
F32 = jnp.float32
BF16 = jnp.bfloat16
TURN = (((1,), (1,)), ((), ()))
IN_VMEM = pl.BlockSpec(memory_space=pltpu.VMEM)
IN_SMEM = pl.BlockSpec(memory_space=pltpu.SMEM)
LIMIT = pltpu.CompilerParams(vmem_limit_bytes=24 * 1024 * 1024)
BRIEF = pl.CostEstimate(flops=0, bytes_accessed=0, transcendentals=0)
LONG = pl.CostEstimate(flops=20_000_000_000, bytes_accessed=0, transcendentals=0)


def swap(value, mask, odd_mask=None):
    total = lax.axis_size(AXES)
    masks = (mask, mask if odd_mask is None else odd_mask)
    return lax.ppermute(value, AXES, [(i, i ^ masks[i % 2]) for i in range(total)])


def after(value, *earlier):
    return lax.optimization_barrier((value, *earlier))[0]


def shifted(value, by):
    length = lax.axis_size("blk")
    return lax.ppermute(value, "blk", [(i, (i + by) % length) for i in range(length)])


def layer_rows(operands, first, cot_first, step, outs, at):
    w = operands[4]
    rows, dst = w[pl.ds(first, step), :], pl.ds(at, step)
    total = None
    for agg, cot, out in zip(operands[:2], operands[2:4], outs):
        pre = lax.dot_general(rows, agg[...], TURN, preferred_element_type=F32)
        s = jax.nn.sigmoid(pre)
        out[dst, :] = (pre * s).astype(BF16)
        slope = s * (1.0 + pre * (1.0 - s))
        grad_pre = (cot[pl.ds(cot_first, step), :].astype(F32) * slope).astype(BF16)
        term = jnp.dot(grad_pre, agg[...], preferred_element_type=F32)
        total = term if total is None else total + term
    return total


def layer(operands, first, cot_first, count, kinds, cost=LONG):
    nodes, width = operands[0].shape
    part = count // len(kinds)
    step = min(128, count)

    def body(*refs):
        operands, outs, grads = refs[:5], refs[5:7], refs[7:]
        for at in range(0, count, step):
            total = layer_rows(operands, first + at, cot_first + at, step, outs, at)
            for k, grad in enumerate(grads):
                if len(grads) == 1:
                    grad[pl.ds(at, step), :] = total.astype(grad.dtype)
                else:
                    grad[...] = total[k * part : (k + 1) * part, :].astype(grad.dtype)

    assert len(kinds) == 1 or count == step
    return pl.pallas_call(
        body,
        out_shape=[jax.ShapeDtypeStruct((count, nodes), BF16)] * 2
        + [jax.ShapeDtypeStruct((part, width), kind) for kind in kinds],
        in_specs=[IN_VMEM] * 5,
        out_specs=[IN_VMEM] * (2 + len(kinds)),
        compiler_params=LIMIT,
        cost_estimate=cost,
        name="layer",
    )(*operands)


def one_hot_rows(me, rows, width):
    slots = width // rows // 2
    owner = jnp.repeat((2 * jnp.arange(slots, dtype=jnp.int32)) ^ me, rows)
    at = owner * rows + jnp.tile(jnp.arange(rows, dtype=jnp.int32), slots)
    return (at[:, None] == jnp.arange(width, dtype=jnp.int32)[None, :]).astype(BF16)


def local_any(features, tiles, tile_cols, tile_count, weight, cotangent):
    total = lax.axis_size(AXES)
    group_len = lax.axis_size("blk")
    position = lax.axis_index("blk")
    me = lax.axis_index(AXES)
    slot_total = tiles.shape[1]
    rows, width = weight.shape
    in_use = jnp.arange(slot_total, dtype=jnp.int32) < tile_count[0]
    columns = tile_cols[0] % group_len

    held = weight
    bit = 2
    while bit < total:
        held = jnp.concatenate([held, swap(held, bit)])
        bit *= 2

    blocks = [(position, features)]
    for offset in range(1, (slot_total - 1) // 2 + 1):
        blocks.append(((position - offset) % group_len, shifted(features, offset)))
        blocks.append(((position + offset) % group_len, shifted(features, -offset)))
    summed = 0.0
    for source, block in blocks:
        match = jnp.logical_and(in_use, columns == source)
        tile = jnp.sum(jnp.where(match[:, None, None], tiles[0], 0), axis=0, dtype=BF16)
        summed = summed + jnp.dot(tile, block, preferred_element_type=F32)
    agg_own = summed.astype(BF16)
    agg_other = swap(agg_own, CORE)

    mine = one_hot_rows(me, rows, width)
    others = one_hot_rows(me ^ CORE, rows, width)
    cot_own = lax.dot_general(mine, cotangent, TURN, preferred_element_type=F32).astype(BF16)
    cot_other = lax.dot_general(others, cotangent, TURN, preferred_element_type=F32).astype(BF16)
    operands = (agg_own, agg_other, cot_own, swap(cot_other, CORE), held)
    out_own, out_other, grad = layer(operands, 0, 0, width // 2, [F32])
    bit = total // 2
    while bit > 1:
        n = grad.shape[0] // 2
        grad = grad[:n] + swap(grad[n:].astype(BF16), bit).astype(F32)
        bit //= 2
    out_t = jnp.concatenate([out_own, swap(out_other, CORE)])
    place = jnp.concatenate([mine, others])
    output = lax.dot_general(out_t, place, (((0,), (0,)), ((), ())), preferred_element_type=F32)
    return output.astype(BF16), grad


def hold_body(weight, near_block, out):
    out[...] = weight[...]


def hold(weight, near_block):
    return pl.pallas_call(
        hold_body,
        out_shape=jax.ShapeDtypeStruct(weight.shape, BF16),
        in_specs=[IN_VMEM, pl.BlockSpec(memory_space=pl.ANY)],
        out_specs=IN_VMEM,
        compiler_params=LIMIT,
        cost_estimate=LONG,
        name="hold",
    )(weight, near_block)


def prepare_body(
    me_ref, cols, count, tiles_in, features_in, cotangent_in, near_block,
    partial, tile_x, cot_own, cot_other, place, tiles, features, cotangent, sems,
):
    copies = [
        pltpu.make_async_copy(src, dst, sems.at[k])
        for k, (src, dst) in enumerate(
            ((tiles_in, tiles), (features_in, features), (cotangent_in, cotangent))
        )
    ]
    for copy in copies:
        copy.start()
    me = me_ref[0]
    core = me % 2
    position = me % 4
    width = features.shape[1]
    half = width // 2
    rows = half // 16

    def tile_of(source):
        chosen = jnp.zeros(tiles.shape[2:], BF16)
        for k in range(tiles.shape[1]):
            match = jnp.logical_and(k < count[0], cols[0, k] % 4 == source)
            chosen = jnp.where(match, tiles[0, k], chosen)
        return chosen

    row_at = lax.broadcasted_iota(jnp.int32, (rows, width), 0)
    column_at = lax.broadcasted_iota(jnp.int32, (rows, width), 1)
    for whose in range(2):
        even = core == whose
        first, second = jnp.where(even, X, Y), jnp.where(even, Y, X)
        for slot in range(16):
            z = ALONG_Z[slot // 8 * 2 + slot % 2]
            mask = (slot // 4 % 2) * first + (slot // 2 % 2) * second + z
            start = (me ^ whose ^ mask) * rows
            at = whose * half + slot * rows
            place[at : at + rows, :] = (column_at == row_at + start).astype(BF16)
    copies[0].wait()
    copies[1].wait()
    tile_x[...] = tile_of(position ^ (X ^ CORE))
    partial[...] = jnp.dot(
        tile_of(position), features[...], preferred_element_type=F32
    ) + jnp.dot(tile_of(position ^ CORE), near_block[...], preferred_element_type=F32)
    copies[2].wait()
    for whose, cot in ((0, cot_own), (1, cot_other)):
        cot[...] = lax.dot_general(
            place[whose * half : (whose + 1) * half, :], cotangent[...], TURN,
            preferred_element_type=F32,
        ).astype(BF16)


def prepare(me, cols, count, tiles, features, cotangent, near_block):
    nodes, width = features.shape
    half = width // 2
    side = tiles.shape[2]
    return pl.pallas_call(
        prepare_body,
        out_shape=[
            jax.ShapeDtypeStruct((nodes, width), F32),
            jax.ShapeDtypeStruct((side, side), BF16),
            jax.ShapeDtypeStruct((half, nodes), BF16),
            jax.ShapeDtypeStruct((half, nodes), BF16),
            jax.ShapeDtypeStruct((width, width), BF16),
        ],
        in_specs=[IN_SMEM] * 3 + [pl.BlockSpec(memory_space=pltpu.HBM)] * 3 + [IN_VMEM],
        out_specs=[IN_VMEM] * 5,
        scratch_shapes=[
            pltpu.VMEM(tiles.shape, BF16),
            pltpu.VMEM(features.shape, BF16),
            pltpu.VMEM(cotangent.shape, BF16),
            pltpu.SemaphoreType.DMA((3,)),
        ],
        compiler_params=LIMIT,
        cost_estimate=BRIEF,
        name="prepare",
    )(me, cols, count, tiles, features, cotangent, near_block)


def aggregate_body(partial, tile, block, out):
    out[...] = (
        partial[...] + jnp.dot(tile[...], block[...], preferred_element_type=F32)
    ).astype(BF16)


def aggregate(partial, tile, block):
    return pl.pallas_call(
        aggregate_body,
        out_shape=jax.ShapeDtypeStruct(partial.shape, BF16),
        in_specs=[IN_VMEM] * 3,
        out_specs=IN_VMEM,
        compiler_params=LIMIT,
        cost_estimate=BRIEF,
        name="aggregate",
    )(partial, tile, block)


def order_body(me_ref, *refs):
    pieces, w = refs[:4], refs[4]
    rows = pieces[0].shape[0] // 2
    even = me_ref[0] % 2 == 0
    for first in range(2):
        for second in range(2):
            for z in range(2):
                by_x = pieces[second * 2 + z][first * rows : (first + 1) * rows, :]
                by_y = pieces[first * 2 + z][second * rows : (second + 1) * rows, :]
                at = ((first * 2 + second) * 2 + z) * rows
                w[at : at + rows, :] = jnp.where(even, by_x, by_y)


def in_order(me, pieces):
    rows, width = pieces[0].shape
    return pl.pallas_call(
        order_body,
        out_shape=jax.ShapeDtypeStruct((4 * rows, width), BF16),
        in_specs=[IN_SMEM] + [IN_VMEM] * 4,
        out_specs=IN_VMEM,
        compiler_params=LIMIT,
        cost_estimate=LONG,
        name="in_order",
    )(me, *pieces)


def into_place_body(*refs):
    parts, place, out = refs[:-2], refs[-2], refs[-1]
    at, total = 0, 0.0
    for part in parts:
        count = part.shape[0]
        total += lax.dot_general(
            part[...], place[at : at + count, :], (((0,), (0,)), ((), ())),
            preferred_element_type=F32,
        )
        at += count
    out[...] = total.astype(out.dtype)


def into_place(parts, place):
    return pl.pallas_call(
        into_place_body,
        out_shape=jax.ShapeDtypeStruct((parts[0].shape[1], place.shape[1]), BF16),
        in_specs=[IN_VMEM] * (len(parts) + 1),
        out_specs=IN_VMEM,
        compiler_params=LIMIT,
        cost_estimate=BRIEF,
        name="into_place",
    )(*parts, place)


def add(kept, first, count, got, kind, cost=BRIEF):
    def body(kept_ref, got_ref, out):
        out[...] = (kept_ref[pl.ds(first, count), :] + got_ref[...].astype(F32)).astype(kind)

    return pl.pallas_call(
        body,
        out_shape=jax.ShapeDtypeStruct((count, kept.shape[1]), kind),
        in_specs=[IN_VMEM] * 2,
        out_specs=IN_VMEM,
        compiler_params=LIMIT,
        cost_estimate=cost,
        name="add",
    )(kept, got)


def local_cube(features, tiles, tile_cols, tile_count, weight, cotangent):
    me = lax.axis_index(AXES).astype(jnp.int32).reshape(1)
    rows, width = weight.shape

    weight_x = swap(weight, X)
    tick = swap(tile_count, CORE)
    x_block = swap(after(features, tick), X ^ CORE)
    pair = jnp.concatenate([hold(weight, tick), weight_x])
    near_block = swap(after(features, tick), CORE)
    far = swap(pair, FAR)
    near = swap(pair, NEAR)
    pieces = {(0, 0): pair, (0, NEAR): near}
    pieces[1, 0] = swap(pair, Y)
    pieces[1, NEAR] = swap(pair, Y ^ NEAR)
    partial, tile_x, cot_own, cot_other, place = prepare(
        after(me, pair), tile_cols, tile_count, tiles, features, cotangent, near_block
    )
    cot_other = swap(after(cot_other, x_block), CORE)
    far = after(far, pieces[1, 0], partial)
    pieces[0, FAR] = far
    pieces[1, FAR] = swap(far, Y)
    pieces[1, NEAR ^ FAR] = swap(far, Y ^ NEAR)

    agg_own = aggregate(partial, tile_x, x_block)
    agg_other = swap(agg_own, CORE)
    pieces[0, NEAR ^ FAR] = swap(after(far, agg_own), NEAR)
    order_e = [pieces[y, z] for y in range(2) for z in ALONG_Z[:2]]
    order_e[0] = after(order_e[0], agg_own)
    w_e = in_order(me, order_e)
    operands = [agg_own, agg_other, cot_own, cot_other]
    half = 2 * rows
    own_e1, other_e1, send_e = layer(operands + [w_e], 2 * half, 2 * half, 2 * half, [BF16])
    got_e = swap(send_e, X, Y)
    order_l = [pieces[y, z] for y in range(2) for z in ALONG_Z[2:]]
    order_l[0] = after(order_l[0], send_e)
    w_l = in_order(me, order_l)
    own_l1, other_l1, send_0, send_1 = layer(
        operands + [w_l], 2 * half, 6 * half, 2 * half, [BF16] * 2
    )
    got_1 = swap(send_1, X, Y)
    got_0 = swap(send_0, X, Y)
    w_e = after(w_e, send_1)
    own_e0, other_e0, keep_e = layer(operands + [w_e], 0, 0, 2 * half, [F32])
    own_l0, other_l0, keep_l = layer(operands + [w_l], 0, 4 * half, 2 * half, [F32])

    send = add(keep_e, half, half, got_e[half:], BF16)
    keep_e = add(keep_e, 0, half, got_e[:half], F32)
    got_e = swap(send, Y, X)

    got_24 = swap(add(keep_l, half, rows, got_1[:rows], BF16), Y, X)
    got_16 = swap(add(keep_l, half + rows, rows, got_1[rows:], BF16), Y, X)
    keep_l = add(keep_l, 0, half, got_0, F32)

    others = jnp.concatenate([other_e0, other_e1, other_l0, other_l1])
    from_other = swap(others, CORE)
    output = into_place([own_e0, own_e1, own_l0, own_l1, from_other], place)

    got_8 = swap(add(keep_e, rows, rows, got_e[rows:], BF16), ALONG_Z[1])
    send_16 = add(keep_l, rows, rows, after(got_16, output), BF16)
    got_16 = swap(send_16, ALONG_Z[3])
    got_24 = after(got_24, output, send_16)
    got_24 = swap(add(keep_l, 0, rows, got_24, BF16), ALONG_Z[2])
    mine = keep_e[:rows] + got_e[:rows].astype(F32)
    return output, mine + sum(v.astype(F32) for v in (got_24, got_16, got_8))


def solution(mesh):
    cube = mesh.shape["rows"] == 8 and mesh.shape["blk"] == 4
    in_specs = (
        P(AXES, None),
        P(AXES, None, None, None),
        P(AXES, None),
        P(AXES),
        P(AXES, None),
        P(AXES, None),
    )
    out_specs = (P(AXES, None), P(AXES, None))
    return jax.shard_map(
        local_cube if cube else local_any,
        mesh=mesh,
        in_specs=in_specs,
        out_specs=out_specs,
        check_vma=False,
    )
```

```python
import jax
import jax.numpy as jnp
from jax import lax
from jax.experimental import pallas as pl
from jax.experimental.pallas import tpu as pltpu
from jax.sharding import PartitionSpec as P

AXES = ("rows", "blk")
CORE, X, Y, NEAR, FAR = 1, 2, 4, 8, 16
ALONG_Z = (0, NEAR, NEAR ^ FAR, FAR)
F32 = jnp.float32
BF16 = jnp.bfloat16
TURN = (((1,), (1,)), ((), ()))
IN_VMEM = pl.BlockSpec(memory_space=pltpu.VMEM)
IN_SMEM = pl.BlockSpec(memory_space=pltpu.SMEM)
LIMIT = pltpu.CompilerParams(vmem_limit_bytes=24 * 1024 * 1024)
BRIEF = pl.CostEstimate(flops=0, bytes_accessed=0, transcendentals=0)
LONG = pl.CostEstimate(flops=20_000_000_000, bytes_accessed=0, transcendentals=0)


def swap(value, mask, odd_mask=None):
    total = lax.axis_size(AXES)
    masks = (mask, mask if odd_mask is None else odd_mask)
    return lax.ppermute(value, AXES, [(i, i ^ masks[i % 2]) for i in range(total)])


def after(value, *earlier):
    return lax.optimization_barrier((value, *earlier))[0]


def shifted(value, by):
    length = lax.axis_size("blk")
    return lax.ppermute(value, "blk", [(i, (i + by) % length) for i in range(length)])


def layer_rows(operands, first, cot_first, step, outs, at):
    w = operands[4]
    rows, dst = w[pl.ds(first, step), :], pl.ds(at, step)
    total = None
    for agg, cot, out in zip(operands[:2], operands[2:4], outs):
        pre = lax.dot_general(rows, agg[...], TURN, preferred_element_type=F32)
        s = jax.nn.sigmoid(pre)
        out[dst, :] = (pre * s).astype(BF16)
        slope = s * (1.0 + pre * (1.0 - s))
        grad_pre = (cot[pl.ds(cot_first, step), :].astype(F32) * slope).astype(BF16)
        term = jnp.dot(grad_pre, agg[...], preferred_element_type=F32)
        total = term if total is None else total + term
    return total


def layer(operands, first, cot_first, count, kinds, cost=LONG):
    nodes, width = operands[0].shape
    part = count // len(kinds)
    step = min(128, count)

    def body(*refs):
        operands, outs, grads = refs[:5], refs[5:7], refs[7:]
        for at in range(0, count, step):
            total = layer_rows(operands, first + at, cot_first + at, step, outs, at)
            for k, grad in enumerate(grads):
                if len(grads) == 1:
                    grad[pl.ds(at, step), :] = total.astype(grad.dtype)
                else:
                    grad[...] = total[k * part : (k + 1) * part, :].astype(grad.dtype)

    assert len(kinds) == 1 or count == step
    return pl.pallas_call(
        body,
        out_shape=[jax.ShapeDtypeStruct((count, nodes), BF16)] * 2
        + [jax.ShapeDtypeStruct((part, width), kind) for kind in kinds],
        in_specs=[IN_VMEM] * 5,
        out_specs=[IN_VMEM] * (2 + len(kinds)),
        compiler_params=LIMIT,
        cost_estimate=cost,
        name="layer",
    )(*operands)


def one_hot_rows(me, rows, width):
    slots = width // rows // 2
    owner = jnp.repeat((2 * jnp.arange(slots, dtype=jnp.int32)) ^ me, rows)
    at = owner * rows + jnp.tile(jnp.arange(rows, dtype=jnp.int32), slots)
    return (at[:, None] == jnp.arange(width, dtype=jnp.int32)[None, :]).astype(BF16)


def local_any(features, tiles, tile_cols, tile_count, weight, cotangent):
    total = lax.axis_size(AXES)
    group_len = lax.axis_size("blk")
    position = lax.axis_index("blk")
    me = lax.axis_index(AXES)
    slot_total = tiles.shape[1]
    rows, width = weight.shape
    in_use = jnp.arange(slot_total, dtype=jnp.int32) < tile_count[0]
    columns = tile_cols[0] % group_len

    held = weight
    bit = 2
    while bit < total:
        held = jnp.concatenate([held, swap(held, bit)])
        bit *= 2

    blocks = [(position, features)]
    for offset in range(1, (slot_total - 1) // 2 + 1):
        blocks.append(((position - offset) % group_len, shifted(features, offset)))
        blocks.append(((position + offset) % group_len, shifted(features, -offset)))
    summed = 0.0
    for source, block in blocks:
        match = jnp.logical_and(in_use, columns == source)
        tile = jnp.sum(jnp.where(match[:, None, None], tiles[0], 0), axis=0, dtype=BF16)
        summed = summed + jnp.dot(tile, block, preferred_element_type=F32)
    agg_own = summed.astype(BF16)
    agg_other = swap(agg_own, CORE)

    mine = one_hot_rows(me, rows, width)
    others = one_hot_rows(me ^ CORE, rows, width)
    cot_own = lax.dot_general(mine, cotangent, TURN, preferred_element_type=F32).astype(BF16)
    cot_other = lax.dot_general(others, cotangent, TURN, preferred_element_type=F32).astype(BF16)
    operands = (agg_own, agg_other, cot_own, swap(cot_other, CORE), held)
    out_own, out_other, grad = layer(operands, 0, 0, width // 2, [F32])
    bit = total // 2
    while bit > 1:
        n = grad.shape[0] // 2
        grad = grad[:n] + swap(grad[n:].astype(BF16), bit).astype(F32)
        bit //= 2
    out_t = jnp.concatenate([out_own, swap(out_other, CORE)])
    place = jnp.concatenate([mine, others])
    output = lax.dot_general(out_t, place, (((0,), (0,)), ((), ())), preferred_element_type=F32)
    return output.astype(BF16), grad


def hold_body(weight, near_block, out):
    out[...] = weight[...]


def hold(weight, near_block):
    return pl.pallas_call(
        hold_body,
        out_shape=jax.ShapeDtypeStruct(weight.shape, BF16),
        in_specs=[IN_VMEM, pl.BlockSpec(memory_space=pl.ANY)],
        out_specs=IN_VMEM,
        compiler_params=LIMIT,
        cost_estimate=LONG,
        name="hold",
    )(weight, near_block)


def prepare_body(
    me_ref, cols, count, tiles_in, features_in, cotangent_in, near_block,
    partial, tile_x, cot_own, cot_other, place, tiles, features, cotangent, sems,
):
    copies = [
        pltpu.make_async_copy(src, dst, sems.at[k])
        for k, (src, dst) in enumerate(
            ((tiles_in, tiles), (features_in, features), (cotangent_in, cotangent))
        )
    ]
    for copy in copies:
        copy.start()
    me = me_ref[0]
    core = me % 2
    position = me % 4
    width = features.shape[1]
    half = width // 2
    rows = half // 16

    def tile_of(source):
        chosen = jnp.zeros(tiles.shape[2:], BF16)
        for k in range(tiles.shape[1]):
            match = jnp.logical_and(k < count[0], cols[0, k] % 4 == source)
            chosen = jnp.where(match, tiles[0, k], chosen)
        return chosen

    row_at = lax.broadcasted_iota(jnp.int32, (rows, width), 0)
    column_at = lax.broadcasted_iota(jnp.int32, (rows, width), 1)
    for whose in range(2):
        even = core == whose
        first, second = jnp.where(even, X, Y), jnp.where(even, Y, X)
        for slot in range(16):
            z = ALONG_Z[slot // 8 * 2 + slot % 2]
            mask = (slot // 4 % 2) * first + (slot // 2 % 2) * second + z
            start = (me ^ whose ^ mask) * rows
            at = whose * half + slot * rows
            place[at : at + rows, :] = (column_at == row_at + start).astype(BF16)
    copies[0].wait()
    copies[1].wait()
    tile_x[...] = tile_of(position ^ (X ^ CORE))
    partial[...] = jnp.dot(
        tile_of(position), features[...], preferred_element_type=F32
    ) + jnp.dot(tile_of(position ^ CORE), near_block[...], preferred_element_type=F32)
    copies[2].wait()
    for whose, cot in ((0, cot_own), (1, cot_other)):
        cot[...] = lax.dot_general(
            place[whose * half : (whose + 1) * half, :], cotangent[...], TURN,
            preferred_element_type=F32,
        ).astype(BF16)


def prepare(me, cols, count, tiles, features, cotangent, near_block):
    nodes, width = features.shape
    half = width // 2
    side = tiles.shape[2]
    return pl.pallas_call(
        prepare_body,
        out_shape=[
            jax.ShapeDtypeStruct((nodes, width), F32),
            jax.ShapeDtypeStruct((side, side), BF16),
            jax.ShapeDtypeStruct((half, nodes), BF16),
            jax.ShapeDtypeStruct((half, nodes), BF16),
            jax.ShapeDtypeStruct((width, width), BF16),
        ],
        in_specs=[IN_SMEM] * 3 + [pl.BlockSpec(memory_space=pltpu.HBM)] * 3 + [IN_VMEM],
        out_specs=[IN_VMEM] * 5,
        scratch_shapes=[
            pltpu.VMEM(tiles.shape, BF16),
            pltpu.VMEM(features.shape, BF16),
            pltpu.VMEM(cotangent.shape, BF16),
            pltpu.SemaphoreType.DMA((3,)),
        ],
        compiler_params=LIMIT,
        cost_estimate=BRIEF,
        name="prepare",
    )(me, cols, count, tiles, features, cotangent, near_block)


def aggregate_body(partial, tile, block, out):
    out[...] = (
        partial[...] + jnp.dot(tile[...], block[...], preferred_element_type=F32)
    ).astype(BF16)


def aggregate(partial, tile, block):
    return pl.pallas_call(
        aggregate_body,
        out_shape=jax.ShapeDtypeStruct(partial.shape, BF16),
        in_specs=[IN_VMEM] * 3,
        out_specs=IN_VMEM,
        compiler_params=LIMIT,
        cost_estimate=BRIEF,
        name="aggregate",
    )(partial, tile, block)


def order_body(me_ref, *refs):
    pieces, w = refs[:4], refs[4]
    rows = pieces[0].shape[0] // 2
    even = me_ref[0] % 2 == 0
    for first in range(2):
        for second in range(2):
            for z in range(2):
                by_x = pieces[second * 2 + z][first * rows : (first + 1) * rows, :]
                by_y = pieces[first * 2 + z][second * rows : (second + 1) * rows, :]
                at = ((first * 2 + second) * 2 + z) * rows
                w[at : at + rows, :] = jnp.where(even, by_x, by_y)


def in_order(me, pieces):
    rows, width = pieces[0].shape
    return pl.pallas_call(
        order_body,
        out_shape=jax.ShapeDtypeStruct((4 * rows, width), BF16),
        in_specs=[IN_SMEM] + [IN_VMEM] * 4,
        out_specs=IN_VMEM,
        compiler_params=LIMIT,
        cost_estimate=LONG,
        name="in_order",
    )(me, *pieces)


def into_place_body(*refs):
    parts, place, out = refs[:-2], refs[-2], refs[-1]
    at, total = 0, 0.0
    for part in parts:
        count = part.shape[0]
        total += lax.dot_general(
            part[...], place[at : at + count, :], (((0,), (0,)), ((), ())),
            preferred_element_type=F32,
        )
        at += count
    out[...] = total.astype(out.dtype)


def into_place(parts, place):
    return pl.pallas_call(
        into_place_body,
        out_shape=jax.ShapeDtypeStruct((parts[0].shape[1], place.shape[1]), BF16),
        in_specs=[IN_VMEM] * (len(parts) + 1),
        out_specs=IN_VMEM,
        compiler_params=LIMIT,
        cost_estimate=BRIEF,
        name="into_place",
    )(*parts, place)


def add(kept, first, count, got, kind, cost=BRIEF):
    def body(kept_ref, got_ref, out):
        out[...] = (kept_ref[pl.ds(first, count), :] + got_ref[...].astype(F32)).astype(kind)

    return pl.pallas_call(
        body,
        out_shape=jax.ShapeDtypeStruct((count, kept.shape[1]), kind),
        in_specs=[IN_VMEM] * 2,
        out_specs=IN_VMEM,
        compiler_params=LIMIT,
        cost_estimate=cost,
        name="add",
    )(kept, got)


def local_cube(features, tiles, tile_cols, tile_count, weight, cotangent):
    me = lax.axis_index(AXES).astype(jnp.int32).reshape(1)
    rows, width = weight.shape

    weight_x = swap(weight, X)
    tick = swap(tile_count, CORE)
    x_block = swap(after(features, tick), X ^ CORE)
    pair = jnp.concatenate([hold(weight, tick), weight_x])
    near_block = swap(after(features, tick), CORE)
    far = swap(pair, FAR)
    near = swap(pair, NEAR)
    pieces = {(0, 0): pair, (0, NEAR): near}
    pieces[1, 0] = swap(pair, Y)
    pieces[1, NEAR] = swap(pair, Y ^ NEAR)
    partial, tile_x, cot_own, cot_other, place = prepare(
        after(me, pair), tile_cols, tile_count, tiles, features, cotangent, near_block
    )
    cot_other = swap(after(cot_other, x_block), CORE)
    far = after(far, pieces[1, 0], partial)
    pieces[0, FAR] = far
    pieces[1, FAR] = swap(far, Y)
    pieces[1, NEAR ^ FAR] = swap(far, Y ^ NEAR)

    agg_own = aggregate(partial, tile_x, x_block)
    agg_other = swap(agg_own, CORE)
    pieces[0, NEAR ^ FAR] = swap(after(far, agg_own), NEAR)
    order_e = [pieces[y, z] for y in range(2) for z in ALONG_Z[:2]]
    order_e[0] = after(order_e[0], agg_own)
    w_e = in_order(me, order_e)
    operands = [agg_own, agg_other, cot_own, cot_other]
    half = 2 * rows
    own_e1, other_e1, send_e = layer(operands + [w_e], 2 * half, 2 * half, 2 * half, [BF16])
    got_e = swap(send_e, X, Y)
    order_l = [pieces[y, z] for y in range(2) for z in ALONG_Z[2:]]
    order_l[0] = after(order_l[0], send_e)
    w_l = in_order(me, order_l)
    own_l1, other_l1, send_0, send_1 = layer(
        operands + [w_l], 2 * half, 6 * half, 2 * half, [BF16] * 2
    )
    got_1 = swap(send_1, X, Y)
    got_0 = swap(send_0, X, Y)
    w_e = after(w_e, send_1)
    own_e0, other_e0, keep_e = layer(operands + [w_e], 0, 0, 2 * half, [F32])
    own_l0, other_l0, keep_l = layer(operands + [w_l], 0, 4 * half, 2 * half, [F32])

    send = add(keep_e, half, half, got_e[half:], BF16)
    keep_e = add(keep_e, 0, half, got_e[:half], F32)
    got_e = swap(send, Y, X)

    got_24 = swap(add(keep_l, half, rows, got_1[:rows], BF16), Y, X)
    got_16 = swap(add(keep_l, half + rows, rows, got_1[rows:], BF16), Y, X)
    keep_l = add(keep_l, 0, half, got_0, F32)

    others = jnp.concatenate([other_e0, other_e1, other_l0, other_l1])
    from_other = swap(others, CORE)
    output = into_place([own_e0, own_e1, own_l0, own_l1, from_other], place)

    got_8 = swap(add(keep_e, rows, rows, got_e[rows:], BF16), ALONG_Z[1])
    send_24 = add(keep_l, 0, rows, after(got_24, output), BF16)
    got_24 = swap(send_24, ALONG_Z[2])
    got_16 = after(got_16, output, send_24)
    got_16 = swap(add(keep_l, rows, rows, got_16, BF16), ALONG_Z[3])
    mine = keep_e[:rows] + got_e[:rows].astype(F32)
    return output, mine + sum(v.astype(F32) for v in (got_24, got_16, got_8))


def solution(mesh):
    cube = mesh.shape["rows"] == 8 and mesh.shape["blk"] == 4
    in_specs = (
        P(AXES, None),
        P(AXES, None, None, None),
        P(AXES, None),
        P(AXES),
        P(AXES, None),
        P(AXES, None),
    )
    out_specs = (P(AXES, None), P(AXES, None))
    return jax.shard_map(
        local_cube if cube else local_any,
        mesh=mesh,
        in_specs=in_specs,
        out_specs=out_specs,
        check_vma=False,
    )
```

```python
import jax
import jax.numpy as jnp
from jax import lax
from jax.experimental import pallas as pl
from jax.experimental.pallas import tpu as pltpu
from jax.sharding import PartitionSpec as P

AXES = ("rows", "blk")
CORE, X, Y, NEAR, FAR = 1, 2, 4, 8, 16
ALONG_Z = (0, NEAR, NEAR ^ FAR, FAR)
F32 = jnp.float32
BF16 = jnp.bfloat16
TURN = (((1,), (1,)), ((), ()))
IN_VMEM = pl.BlockSpec(memory_space=pltpu.VMEM)
IN_SMEM = pl.BlockSpec(memory_space=pltpu.SMEM)
LIMIT = pltpu.CompilerParams(vmem_limit_bytes=24 * 1024 * 1024)
BRIEF = pl.CostEstimate(flops=0, bytes_accessed=0, transcendentals=0)
LONG = pl.CostEstimate(flops=20_000_000_000, bytes_accessed=0, transcendentals=0)


def swap(value, mask, odd_mask=None):
    total = lax.axis_size(AXES)
    masks = (mask, mask if odd_mask is None else odd_mask)
    return lax.ppermute(value, AXES, [(i, i ^ masks[i % 2]) for i in range(total)])


def after(value, *earlier):
    return lax.optimization_barrier((value, *earlier))[0]


def shifted(value, by):
    length = lax.axis_size("blk")
    return lax.ppermute(value, "blk", [(i, (i + by) % length) for i in range(length)])


def layer_rows(operands, first, cot_first, step, outs, at):
    w = operands[4]
    rows, dst = w[pl.ds(first, step), :], pl.ds(at, step)
    total = None
    for agg, cot, out in zip(operands[:2], operands[2:4], outs):
        pre = lax.dot_general(rows, agg[...], TURN, preferred_element_type=F32)
        s = jax.nn.sigmoid(pre)
        out[dst, :] = (pre * s).astype(BF16)
        slope = s * (1.0 + pre * (1.0 - s))
        grad_pre = (cot[pl.ds(cot_first, step), :].astype(F32) * slope).astype(BF16)
        term = jnp.dot(grad_pre, agg[...], preferred_element_type=F32)
        total = term if total is None else total + term
    return total


def layer(operands, first, cot_first, count, kinds, cost=LONG):
    nodes, width = operands[0].shape
    part = count // len(kinds)
    step = min(128, count)

    def body(*refs):
        operands, outs, grads = refs[:5], refs[5:7], refs[7:]
        for at in range(0, count, step):
            total = layer_rows(operands, first + at, cot_first + at, step, outs, at)
            for k, grad in enumerate(grads):
                if len(grads) == 1:
                    grad[pl.ds(at, step), :] = total.astype(grad.dtype)
                else:
                    grad[...] = total[k * part : (k + 1) * part, :].astype(grad.dtype)

    assert len(kinds) == 1 or count == step
    return pl.pallas_call(
        body,
        out_shape=[jax.ShapeDtypeStruct((count, nodes), BF16)] * 2
        + [jax.ShapeDtypeStruct((part, width), kind) for kind in kinds],
        in_specs=[IN_VMEM] * 5,
        out_specs=[IN_VMEM] * (2 + len(kinds)),
        compiler_params=LIMIT,
        cost_estimate=cost,
        name="layer",
    )(*operands)


def one_hot_rows(me, rows, width):
    slots = width // rows // 2
    owner = jnp.repeat((2 * jnp.arange(slots, dtype=jnp.int32)) ^ me, rows)
    at = owner * rows + jnp.tile(jnp.arange(rows, dtype=jnp.int32), slots)
    return (at[:, None] == jnp.arange(width, dtype=jnp.int32)[None, :]).astype(BF16)


def local_any(features, tiles, tile_cols, tile_count, weight, cotangent):
    total = lax.axis_size(AXES)
    group_len = lax.axis_size("blk")
    position = lax.axis_index("blk")
    me = lax.axis_index(AXES)
    slot_total = tiles.shape[1]
    rows, width = weight.shape
    in_use = jnp.arange(slot_total, dtype=jnp.int32) < tile_count[0]
    columns = tile_cols[0] % group_len

    held = weight
    bit = 2
    while bit < total:
        held = jnp.concatenate([held, swap(held, bit)])
        bit *= 2

    blocks = [(position, features)]
    for offset in range(1, (slot_total - 1) // 2 + 1):
        blocks.append(((position - offset) % group_len, shifted(features, offset)))
        blocks.append(((position + offset) % group_len, shifted(features, -offset)))
    summed = 0.0
    for source, block in blocks:
        match = jnp.logical_and(in_use, columns == source)
        tile = jnp.sum(jnp.where(match[:, None, None], tiles[0], 0), axis=0, dtype=BF16)
        summed = summed + jnp.dot(tile, block, preferred_element_type=F32)
    agg_own = summed.astype(BF16)
    agg_other = swap(agg_own, CORE)

    mine = one_hot_rows(me, rows, width)
    others = one_hot_rows(me ^ CORE, rows, width)
    cot_own = lax.dot_general(mine, cotangent, TURN, preferred_element_type=F32).astype(BF16)
    cot_other = lax.dot_general(others, cotangent, TURN, preferred_element_type=F32).astype(BF16)
    operands = (agg_own, agg_other, cot_own, swap(cot_other, CORE), held)
    out_own, out_other, grad = layer(operands, 0, 0, width // 2, [F32])
    bit = total // 2
    while bit > 1:
        n = grad.shape[0] // 2
        grad = grad[:n] + swap(grad[n:].astype(BF16), bit).astype(F32)
        bit //= 2
    out_t = jnp.concatenate([out_own, swap(out_other, CORE)])
    place = jnp.concatenate([mine, others])
    output = lax.dot_general(out_t, place, (((0,), (0,)), ((), ())), preferred_element_type=F32)
    return output.astype(BF16), grad


def hold_body(weight, near_block, out):
    out[...] = weight[...]


def hold(weight, near_block):
    return pl.pallas_call(
        hold_body,
        out_shape=jax.ShapeDtypeStruct(weight.shape, BF16),
        in_specs=[IN_VMEM, pl.BlockSpec(memory_space=pl.ANY)],
        out_specs=IN_VMEM,
        compiler_params=LIMIT,
        cost_estimate=LONG,
        name="hold",
    )(weight, near_block)


def prepare_body(
    me_ref, cols, count, tiles_in, features_in, cotangent_in, near_block,
    partial, tile_x, cot_own, cot_other, place, tiles, features, cotangent, sems,
):
    copies = [
        pltpu.make_async_copy(src, dst, sems.at[k])
        for k, (src, dst) in enumerate(
            ((tiles_in, tiles), (features_in, features), (cotangent_in, cotangent))
        )
    ]
    for copy in copies:
        copy.start()
    me = me_ref[0]
    core = me % 2
    position = me % 4
    width = features.shape[1]
    half = width // 2
    rows = half // 16

    def tile_of(source):
        chosen = jnp.zeros(tiles.shape[2:], BF16)
        for k in range(tiles.shape[1]):
            match = jnp.logical_and(k < count[0], cols[0, k] % 4 == source)
            chosen = jnp.where(match, tiles[0, k], chosen)
        return chosen

    row_at = lax.broadcasted_iota(jnp.int32, (rows, width), 0)
    column_at = lax.broadcasted_iota(jnp.int32, (rows, width), 1)
    for whose in range(2):
        even = core == whose
        first, second = jnp.where(even, X, Y), jnp.where(even, Y, X)
        for slot in range(16):
            z = ALONG_Z[slot // 8 * 2 + slot % 2]
            mask = (slot // 4 % 2) * first + (slot // 2 % 2) * second + z
            start = (me ^ whose ^ mask) * rows
            at = whose * half + slot * rows
            place[at : at + rows, :] = (column_at == row_at + start).astype(BF16)
    copies[0].wait()
    copies[1].wait()
    tile_x[...] = tile_of(position ^ (X ^ CORE))
    partial[...] = jnp.dot(
        tile_of(position), features[...], preferred_element_type=F32
    ) + jnp.dot(tile_of(position ^ CORE), near_block[...], preferred_element_type=F32)
    copies[2].wait()
    for whose, cot in ((0, cot_own), (1, cot_other)):
        cot[...] = lax.dot_general(
            place[whose * half : (whose + 1) * half, :], cotangent[...], TURN,
            preferred_element_type=F32,
        ).astype(BF16)


def prepare(me, cols, count, tiles, features, cotangent, near_block):
    nodes, width = features.shape
    half = width // 2
    side = tiles.shape[2]
    return pl.pallas_call(
        prepare_body,
        out_shape=[
            jax.ShapeDtypeStruct((nodes, width), F32),
            jax.ShapeDtypeStruct((side, side), BF16),
            jax.ShapeDtypeStruct((half, nodes), BF16),
            jax.ShapeDtypeStruct((half, nodes), BF16),
            jax.ShapeDtypeStruct((width, width), BF16),
        ],
        in_specs=[IN_SMEM] * 3 + [pl.BlockSpec(memory_space=pltpu.HBM)] * 3 + [IN_VMEM],
        out_specs=[IN_VMEM] * 5,
        scratch_shapes=[
            pltpu.VMEM(tiles.shape, BF16),
            pltpu.VMEM(features.shape, BF16),
            pltpu.VMEM(cotangent.shape, BF16),
            pltpu.SemaphoreType.DMA((3,)),
        ],
        compiler_params=LIMIT,
        cost_estimate=BRIEF,
        name="prepare",
    )(me, cols, count, tiles, features, cotangent, near_block)


def aggregate_body(partial, tile, block, out):
    out[...] = (
        partial[...] + jnp.dot(tile[...], block[...], preferred_element_type=F32)
    ).astype(BF16)


def aggregate(partial, tile, block):
    return pl.pallas_call(
        aggregate_body,
        out_shape=jax.ShapeDtypeStruct(partial.shape, BF16),
        in_specs=[IN_VMEM] * 3,
        out_specs=IN_VMEM,
        compiler_params=LIMIT,
        cost_estimate=BRIEF,
        name="aggregate",
    )(partial, tile, block)


def order_body(me_ref, *refs):
    pieces, w = refs[:4], refs[4]
    rows = pieces[0].shape[0] // 2
    even = me_ref[0] % 2 == 0
    for first in range(2):
        for second in range(2):
            for z in range(2):
                by_x = pieces[second * 2 + z][first * rows : (first + 1) * rows, :]
                by_y = pieces[first * 2 + z][second * rows : (second + 1) * rows, :]
                at = ((first * 2 + second) * 2 + z) * rows
                w[at : at + rows, :] = jnp.where(even, by_x, by_y)


def in_order(me, pieces):
    rows, width = pieces[0].shape
    return pl.pallas_call(
        order_body,
        out_shape=jax.ShapeDtypeStruct((4 * rows, width), BF16),
        in_specs=[IN_SMEM] + [IN_VMEM] * 4,
        out_specs=IN_VMEM,
        compiler_params=LIMIT,
        cost_estimate=LONG,
        name="in_order",
    )(me, *pieces)


def into_place_body(*refs):
    parts, place, out = refs[:-2], refs[-2], refs[-1]
    at, total = 0, 0.0
    for part in parts:
        count = part.shape[0]
        total += lax.dot_general(
            part[...], place[at : at + count, :], (((0,), (0,)), ((), ())),
            preferred_element_type=F32,
        )
        at += count
    out[...] = total.astype(out.dtype)


def into_place(parts, place):
    return pl.pallas_call(
        into_place_body,
        out_shape=jax.ShapeDtypeStruct((parts[0].shape[1], place.shape[1]), BF16),
        in_specs=[IN_VMEM] * (len(parts) + 1),
        out_specs=IN_VMEM,
        compiler_params=LIMIT,
        cost_estimate=BRIEF,
        name="into_place",
    )(*parts, place)


def add(kept, first, count, got, kind, cost=BRIEF, got_first=0):
    def body(kept_ref, got_ref, out):
        out[...] = (kept_ref[pl.ds(first, count), :] + got_ref[pl.ds(got_first, count), :].astype(F32)).astype(kind)

    return pl.pallas_call(
        body,
        out_shape=jax.ShapeDtypeStruct((count, kept.shape[1]), kind),
        in_specs=[IN_VMEM] * 2,
        out_specs=IN_VMEM,
        compiler_params=LIMIT,
        cost_estimate=cost,
        name="add",
    )(kept, got)


def local_cube(features, tiles, tile_cols, tile_count, weight, cotangent):
    me = lax.axis_index(AXES).astype(jnp.int32).reshape(1)
    rows, width = weight.shape

    weight_x = swap(weight, X)
    tick = swap(tile_count, CORE)
    x_block = swap(after(features, tick), X ^ CORE)
    pair = jnp.concatenate([hold(weight, tick), weight_x])
    near_block = swap(after(features, tick), CORE)
    far = swap(pair, FAR)
    near = swap(pair, NEAR)
    pieces = {(0, 0): pair, (0, NEAR): near}
    pieces[1, 0] = swap(pair, Y)
    pieces[1, NEAR] = swap(pair, Y ^ NEAR)
    partial, tile_x, cot_own, cot_other, place = prepare(
        after(me, pair), tile_cols, tile_count, tiles, features, cotangent, near_block
    )
    cot_other = swap(after(cot_other, x_block), CORE)
    far = after(far, pieces[1, 0], partial)
    pieces[0, FAR] = far
    pieces[1, FAR] = swap(far, Y)
    pieces[1, NEAR ^ FAR] = swap(far, Y ^ NEAR)

    agg_own = aggregate(partial, tile_x, x_block)
    agg_other = swap(agg_own, CORE)
    pieces[0, NEAR ^ FAR] = swap(after(far, agg_own), NEAR)
    order_e = [pieces[y, z] for y in range(2) for z in ALONG_Z[:2]]
    order_e[0] = after(order_e[0], agg_own)
    w_e = in_order(me, order_e)
    operands = [agg_own, agg_other, cot_own, cot_other]
    half = 2 * rows
    own_e1, other_e1, send_e = layer(operands + [w_e], 2 * half, 2 * half, 2 * half, [BF16])
    got_e = swap(send_e, X, Y)
    order_l = [pieces[y, z] for y in range(2) for z in ALONG_Z[2:]]
    order_l[0] = after(order_l[0], send_e)
    w_l = in_order(me, order_l)
    own_l1, other_l1, send_0, send_1 = layer(
        operands + [w_l], 2 * half, 6 * half, 2 * half, [BF16] * 2
    )
    got_1 = swap(send_1, X, Y)
    got_0 = swap(send_0, X, Y)
    w_e = after(w_e, send_1)
    own_e0, other_e0, keep_e = layer(operands + [w_e], 0, 0, 2 * half, [F32])
    own_l0, other_l0, keep_l = layer(operands + [w_l], 0, 4 * half, 2 * half, [F32])

    send = add(keep_e, half, half, got_e, BF16, got_first=half)
    keep_e = add(keep_e, 0, half, got_e, F32)
    got_e = swap(send, Y, X)

    got_24 = swap(add(keep_l, half, rows, got_1, BF16), Y, X)
    got_16 = swap(add(keep_l, half + rows, rows, got_1, BF16, got_first=rows), Y, X)
    keep_l = add(keep_l, 0, half, got_0, F32)

    others = jnp.concatenate([other_e0, other_e1, other_l0, other_l1])
    from_other = swap(others, CORE)
    output = into_place([own_e0, own_e1, own_l0, own_l1, from_other], place)

    got_8 = swap(add(keep_e, rows, rows, got_e, BF16, got_first=rows), ALONG_Z[1])
    send_24 = add(keep_l, 0, rows, after(got_24, output), BF16)
    got_24 = swap(send_24, ALONG_Z[2])
    got_16 = after(got_16, output, send_24)
    got_16 = swap(add(keep_l, rows, rows, got_16, BF16), ALONG_Z[3])
    mine = keep_e[:rows] + got_e[:rows].astype(F32)
    return output, mine + sum(v.astype(F32) for v in (got_24, got_16, got_8))


def solution(mesh):
    cube = mesh.shape["rows"] == 8 and mesh.shape["blk"] == 4
    in_specs = (
        P(AXES, None),
        P(AXES, None, None, None),
        P(AXES, None),
        P(AXES),
        P(AXES, None),
        P(AXES, None),
    )
    out_specs = (P(AXES, None), P(AXES, None))
    return jax.shard_map(
        local_cube if cube else local_any,
        mesh=mesh,
        in_specs=in_specs,
        out_specs=out_specs,
        check_vma=False,
    )
```
